256 devices in a mesh: rep: 16 (over z_hi, x), shard: 16 (over y, z_lo, core).
Axes of the slice: x: 4, y: 4, z: 8 (z_hi: 4, z_lo: 2; z = z_hi * 2 + z_lo), core: 2. Of those that a mesh axis runs over, the one named last changes fastest.
Arguments:
- inputs: bfloat16 [131072, 4608], P(('rep', 'shard')), may hold values from -6 to 6
- gain: bfloat16 [4608], P('shard'), may hold values from -0.5 to 0.5
- weight: bfloat16 [4608, 1024], P('shard'), may hold values from -0.09375 to 0.09375
- upstream: bfloat16 [131072, 1024], P(('rep', 'shard')), may hold values from -6 to 6
Outputs:
- input_grad: bfloat16 [131072, 4608], P(('rep', 'shard'))
- weight_grad: float32 [4608, 1024], P('shard')
- gain_grad: float32 [4608], P('shard')
The draws below stay inside these ranges and needn't reach their ends.
All inputs are finite; a program needn't handle non-finite values.
Results may differ from the reference program's by a relative error of at most 0.0028.
Values may be sent and summed in bfloat16 or wider, within the bound.
A program may use at most 128 MiB of HBM per device.

```python
import math
import jax
import jax.numpy as jnp
from jax import lax

D = 4608
TOK_DEV = 512
COLS = 1024
TOKENS = 131072


def block_levels(key, dims, cuts, smallest, largest):
    level = 1.0
    for dim, blocks in cuts:
        heights = jax.random.uniform(jax.random.fold_in(jax.random.fold_in(key, 6), dim), (blocks,), jnp.float32, smallest / len(cuts), largest / len(cuts))
        level = level * jnp.repeat(jnp.exp(heights), dims[dim] // blocks).reshape((-1,) + (1,) * (len(dims) - 1 - dim))
    return level


def bell_draw(rng, dims, scale, bound, cuts=(), kind=jnp.bfloat16):
    factor_of = block_levels(rng, dims, cuts, -0.22, 0.18) if cuts else 1.0
    drawn = jax.random.normal(rng, dims, jnp.float32) * scale * factor_of
    return jnp.minimum(jnp.maximum(drawn, -bound), bound).astype(kind)


def setup_inputs(seed: int = 0) -> dict:
    key_list = jax.random.split(jax.random.key(seed), 5)
    return {
        "inputs": bell_draw(key_list[0], (TOKENS, D), 1.0, 6.0, ((0, 256),)),
        "gain": jnp.clip(jax.random.uniform(key_list[1], (D,), jnp.float32, -0.5, 0.5) * block_levels(key_list[1], (D,), ((0, 16),), -0.4, 0.0), -0.5, 0.5).astype(jnp.bfloat16),
        "weight": bell_draw(key_list[2], (D, COLS), D ** -0.5, 0.09375, ((0, 16),)),
        "upstream": bell_draw(key_list[3], (TOKENS, COLS), 1.0, 6.0, ((0, 256),)),
    }


def reference(inputs, gain, weight, upstream):
    blocks = TOKENS // TOK_DEV
    scale_gain = 1.0 + gain.astype(jnp.float32)
    xs = inputs.reshape(blocks, TOK_DEV, D)
    ys = upstream.reshape(blocks, TOK_DEV, COLS)

    def step(carry, pair):
        wsum, gsum = carry
        block_x, block_y = pair
        floats = block_x.astype(jnp.float32)
        inverse = lax.rsqrt(lax.optimization_barrier(jnp.mean(floats * floats, axis=-1, keepdims=True)) + 1e-06)
        normed = floats * inverse
        hidden = (normed * scale_gain).astype(jnp.bfloat16)
        delta = lax.dot_general(block_y, weight, (((1,), (1,)), ((), ())), preferred_element_type=jnp.float32)
        scaled = delta * scale_gain
        grad_in = (inverse * (scaled - normed * lax.optimization_barrier(jnp.mean(scaled * normed, axis=-1, keepdims=True)))).astype(jnp.bfloat16)
        wsum = wsum + lax.dot_general(hidden, block_y, (((0,), (0,)), ((), ())), preferred_element_type=jnp.float32)
        gsum = gsum + lax.optimization_barrier(jnp.sum(delta * normed, axis=0))
        return ((wsum, gsum), grad_in)
    start = (jnp.zeros((D, COLS), jnp.float32), jnp.zeros((D,), jnp.float32))
    (wsum, gsum), grads = lax.scan(step, start, (xs, ys))
    factor = 1.0 / math.sqrt(TOKENS)
    return (grads.reshape(TOKENS, D), wsum * factor, gsum * factor)
```

```python
import math

import jax
import jax.numpy as jnp
from jax import lax
from jax.experimental import pallas as pl
from jax.experimental.pallas import tpu as pltpu
from jax.sharding import PartitionSpec as P

MESH = pl.DeviceIdType.MESH
F32 = jnp.float32
BF16 = jnp.bfloat16
TOK = 512
D = 4608
COLS = 1024
ROWS = 288
HALF = D // 2
SUB = 384
QUART = COLS // 4
PAD = D + 128
STRIP = 48
CHUNK = 4 * STRIP
CHUNKS = HALF // CHUNK
STRIPS = ROWS // STRIP
HOLD = 5
FACTOR = 1.0 / math.sqrt(131072)


def ds(start, size, unit):
    return pl.ds(pl.multiple_of(start, unit), size)


def remote(src, dst, send, recv, device):
    return pltpu.make_async_remote_copy(
        src_ref=src, dst_ref=dst, send_sem=send, recv_sem=recv, device_id=device, device_id_type=MESH
    )


def each(first, last, step):
    def body(t, carry):
        step(t)
        return carry

    lax.fori_loop(first, last, body, 0)


def kernel(
    x_hbm, gain, w_hbm, u_hbm,
    ig, wg, gg,
    xv, wv, sv, ht, hs, ups, inv, rd, gfull, gsum, gbuf, gone, gtwo, gmine, win,
    part, s1, l1, r1, s2, l2, r2, s3, r3, zs, zr, fb, ar,
    ld_x, ld_u, ld_w,
    gb_s, gb_r, g1_s, g1_r, g2_s, g2_r,
    u_s, u_r, h_s, h_r,
    wy_s, wy_r, wz_s, wz_r, wc_s, wc_r,
    s1_s, s1_r, s2_s, s2_r, s3_s, s3_r, z_s, z_r, a_s, a_r, b_s, b_r,
):
    rep = lax.axis_index("rep")
    me = lax.axis_index("shard")
    x, zhi = rep % 4, rep // 4
    y, zlo, c = me // 4, (me // 2) % 2, me % 2
    z = zhi * 2 + zlo

    def dev(xx, yy, zz, cc):
        return ((zz // 2) * 4 + xx, (yy * 2 + zz % 2) * 2 + cc)

    sib = (rep, me + 1 - 2 * c)
    right, left = dev((x + 1) % 4, y, z, c), dev((x + 3) % 4, y, z, c)
    up, down = dev(x, y, (z + 1) % 8, c), dev(x, y, (z + 7) % 8, c)

    row = jnp.concatenate([gain[...].astype(F32).reshape(1, ROWS), jnp.zeros((1, 512 - ROWS), F32)], axis=1)
    win[...] = pltpu.roll(jnp.broadcast_to(row, (8, 512)), (32 * me) % 128, 1)[:1]

    def load_x(k):
        rows = ds(k * 64, 64, 64)
        return pltpu.make_async_copy(x_hbm.at[rows, :], xv.at[rows, :], ld_x.at[k])

    each(0, 8, lambda k: load_x(k).start())
    own_tok = ds(c * TOK, TOK, TOK)
    load_u = pltpu.make_async_copy(u_hbm, ups.at[own_tok, :], ld_u)
    load_u.start()
    own_rows = ds(me * ROWS, ROWS, 32)
    load_w = pltpu.make_async_copy(w_hbm, wv.at[own_rows, :], ld_w)
    load_w.start()

    barrier = pltpu.get_barrier_semaphore()

    def hello(device):
        pl.semaphore_signal(barrier, inc=1, device_id=device, device_id_type=MESH)

    each(1, 16, lambda t: hello((rep, (me + t) % 16)))
    each(1, 16, lambda t: hello(((rep + t) % 16, me)))
    each(1, 4, lambda t: hello((((zhi + t) % 4) * 4 + x, (y * 2 + 1 - zlo) * 2 + c)))
    def norm_block(k):
        load_x(k).wait()
        rows = ds(k * 64, 64, 64)
        total = jnp.zeros((64, 128), F32)
        for j in range(D // 512):
            v = xv[rows, j * 512:(j + 1) * 512].astype(F32)
            v = v * v
            total = total + ((v[:, :128] + v[:, 128:256]) + (v[:, 256:384] + v[:, 384:]))
        mean = jnp.sum(total, axis=-1, keepdims=True) * (1.0 / D)
        inv[rows, :] = jnp.broadcast_to(lax.rsqrt(mean + 1e-06), (64, 128))

    each(0, 8, norm_block)

    pl.semaphore_wait(barrier, 33)

    def gain_copy(t):
        return remote(win, gbuf.at[me], gb_s.at[t], gb_r.at[t], (rep, (me + t) % 16))

    each(1, 16, lambda t: gain_copy(t).start())
    gbuf[me] = win[...]
    u_copy = remote(u_hbm, ups.at[own_tok, :], u_s, u_r, sib)
    u_copy.start()

    def w_half(d, zl, cc, h):
        return ds(((((y + d) % 4) * 2 + zl) * 2 + cc) * ROWS + h * 144, 144, 16)

    def y_own(way, h):
        rows = w_half(0, zlo, c, h)
        to = dev(x, (y + (1 if way == 0 else 3)) % 4, z, c)
        return remote(wv.at[rows, :], wv.at[rows, :], wy_s.at[way, h], wy_r.at[way, h], to)

    def y_pass(way):
        rows = w_half(3 if way == 0 else 1, zlo, c, way)
        to = dev(x, (y + (1 if way == 0 else 3)) % 4, z, c)
        return remote(wv.at[rows, :], wv.at[rows, :], wy_s.at[2, way], wy_r.at[2, way], to)

    def z_half(d, h):
        rows = w_half(d, zlo, c, h)
        return remote(wv.at[rows, :], wv.at[rows, :], wz_s.at[d, h], wz_r.at[d, h], up if h == 0 else down)

    def c_half(d, h, k):
        rows = w_half(d, zlo if k == 0 else 1 - zlo, c, h)
        return remote(wv.at[rows, :], wv.at[rows, :], wc_s.at[d, h, k], wc_r.at[d, h, k], sib)

    def arrive(rows, sem):
        remote(wv.at[rows, :], wv.at[rows, :], wc_s.at[0, 0, 0], sem, sib).wait_recv()

    def w_have(d, h):
        z_half(d, h).start()
        c_half(d, h, 0).start()

    def w_near(h, k):
        way = h if k == 0 else 1 - h
        d = 3 if way == 0 else 1
        arrive(w_half(d, zlo, c, h), wy_r.at[way, h])
        if k == 0:
            y_pass(way).start()
        w_have(d, h)

    def w_far(h):
        arrive(w_half(2, zlo, c, h), wy_r.at[2, h])
        w_have(2, h)

    def w_other(d, h):
        arrive(w_half(d, 1 - zlo, c, h), wz_r.at[d, h])
        c_half(d, h, 1).start()

    load_w.wait()
    for way in (0, 1):
        y_own(way, way).start()
        w_have(0, way)
    for way in (0, 1):
        y_own(way, 1 - way).start()

    def gain_wait(t):
        remote(win, gbuf.at[(me + 16 - t) % 16], gb_s.at[t], gb_r.at[t], sib).wait_recv()

    each(1, 16, gain_wait)
    gfull[...] = jnp.ones((1, PAD), F32)
    for s in range(16):
        at = (ROWS * s) // 128 * 128
        gfull[:, at:at + 512] = gfull[:, at:at + 512] + gbuf[s]

    def inv3(rows):
        iv = inv[rows, :]
        return jnp.concatenate([iv, iv, iv], axis=1)

    def hidden_block(j, at_feature, out, at_lane):
        feats = ds(at_feature + j * SUB, SUB, 128)
        scale = gfull[:, feats]

        def tokens(k):
            rows = ds(k * 128, 128, 128)
            v = xv[rows, feats].astype(F32) * inv3(rows)
            v = (v * scale).astype(BF16).T
            for e in range(SUB // STRIP):
                strip = j * (SUB // STRIP) + e
                shard, nth = strip // STRIPS, strip % STRIPS
                to = ((shard // 4) * STRIPS + nth) * CHUNK + ((shard % 2) * 2 + (shard // 2) % 2) * STRIP
                out[ds(to, STRIP, 16), ds(at_lane + k * 128, 128, 128)] = v[e * STRIP:(e + 1) * STRIP]

        each(0, 4, tokens)

    def h_copy(j):
        rows = ds(j * CHUNK, CHUNK, CHUNK)
        return remote(hs.at[rows, :], ht.at[rows, own_tok], h_s.at[j], h_r.at[j], sib)

    def h_wait(j):
        rows = ds(j * CHUNK, CHUNK, CHUNK)
        remote(hs.at[rows, :], ht.at[rows, ds((1 - c) * TOK, TOK, TOK)], h_s.at[j], h_r.at[j], sib).wait_recv()

    def hidden_other(j):
        hidden_block(j, (1 - c) * HALF, hs, 0)

    def hidden_own(j):
        hidden_block(j, c * HALF, ht, c * TOK)

    each(0, 3, hidden_other)
    each(0, STRIPS, lambda j: h_copy(j).start())
    each(0, 3, hidden_own)
    load_u.wait()
    remote(u_hbm, ups.at[ds((1 - c) * TOK, TOK, TOK), :], u_s, u_r, sib).wait_recv()

    rd[...] = jnp.zeros_like(rd)
    gsum[...] = jnp.zeros_like(gsum)

    def delta(d):
        for h in range(2):
            for k in range(2):
                arrive(w_half(d, zlo if k == 0 else 1 - zlo, 1 - c, h), wc_r.at[d, h, k])

        def block(j):
            at = ((y + d) % 4) * 1152 + j * SUB
            feats = ds(at, SUB, 128)
            sv[:, feats] = lax.dot_general(
                ups[own_tok, :], wv[ds(at, SUB, 32), :], (((1,), (1,)), ((), ())), preferred_element_type=F32
            )
            scale = gfull[:, feats]

            def tokens(k, col):
                rows = ds(k * 64, 64, 64)
                dl = sv[rows, feats]
                nm = xv[rows, feats].astype(F32) * inv3(rows)
                dn = dl * nm
                sn = dn * scale
                sv[rows, feats] = dl * scale
                rd[rows, :] = rd[rows, :] + (sn[:, :128] + sn[:, 128:256] + sn[:, 256:])
                return col + jnp.sum(dn.reshape(8, 8, SUB), axis=0)

            col = lax.fori_loop(0, 8, tokens, jnp.zeros((8, SUB), F32))
            gsum[:, feats] = jnp.sum(col, axis=0, keepdims=True)

        each(0, 3, block)

    def finish():
        def mean(k):
            rows = ds(k * 64, 64, 64)
            m = jnp.sum(rd[rows, :], axis=-1, keepdims=True) * (1.0 / D)
            rd[rows, :] = jnp.broadcast_to(m, (64, 128))

        each(0, 8, mean)

        def block(j):
            rows = ds(j * 64, 64, 64)

            def part_of(k):
                feats = ds(k * SUB, SUB, 128)
                iv = inv3(rows)
                m = rd[rows, :]
                nm = xv[rows, feats].astype(F32) * iv
                ig[rows, feats] = (iv * (sv[rows, feats] - nm * jnp.concatenate([m, m, m], axis=1))).astype(BF16)

            each(0, 12, part_of)

        each(0, 8, block)

    def gain_window(s):
        return ds(s * ROWS - (32 * s) % 128, 512, 128)

    def g1_copy(t):
        to = (me + t) % 16
        return remote(gsum.at[:, gain_window(to)], gone.at[me], g1_s.at[t], g1_r.at[t], (rep, to))

    def g1_wait(t):
        remote(gmine, gone.at[(me + 16 - t) % 16], g1_s.at[t], g1_r.at[t], sib).wait_recv()

    def g2_copy(t):
        return remote(gmine, gtwo.at[rep], g2_s.at[t], g2_r.at[t], ((rep + t) % 16, me))

    def g2_wait(t):
        remote(gmine, gtwo.at[(rep + 16 - t) % 16], g2_s.at[t], g2_r.at[t], sib).wait_recv()

    def gain_first():
        each(1, 16, lambda t: g1_copy(t).start())
        gone[me] = gsum[:, gain_window(me)]

    def gain_second():
        each(1, 16, g1_wait)
        total = gone[0]
        for s in range(1, 16):
            total = total + gone[s]
        gmine[...] = total
        gtwo[rep] = total
        each(1, 16, lambda t: g2_copy(t).start())

    def gain_third():
        each(1, 16, g2_wait)
        total = gtwo[0]
        for s in range(1, 16):
            total = total + gtwo[s]
        total = jnp.broadcast_to(total * FACTOR, (8, 512))
        gg[...] = pltpu.roll(total, (512 - (32 * me) % 128) % 512, 1)[0, :ROWS]

    def s1_copy(j, h):
        return remote(s1.at[j, h], (l1 if h == 0 else r1).at[j], s1_s.at[j, h], s1_r.at[j, h], right if h == 0 else left)

    def s1_wait(j, h):
        remote(s1.at[j, h], (l1 if h == 0 else r1).at[j], s1_s.at[j, h], s1_r.at[j, h], left).wait_recv()

    def s2_copy(j, h):
        return remote(s2.at[j, h], (l2 if h == 0 else r2).at[j], s2_s.at[j, h], s2_r.at[j, h], right if h == 0 else left)

    def s2_wait(j, h):
        remote(s2.at[j, h], (l2 if h == 0 else r2).at[j], s2_s.at[j, h], s2_r.at[j, h], left).wait_recv()

    def matmul(j):
        h_wait(j)
        slot = j % HOLD
        rows = ds(j * CHUNK, CHUNK, CHUNK)

        def quarter(q):
            return jnp.dot(ht[rows, :], ups[:, ds(q * QUART, QUART, 128)], preferred_element_type=F32)

        far = quarter((x + 2) % 4).astype(BF16)
        s1[j, 0] = far[:CHUNK // 2]
        s1[j, 1] = far[CHUNK // 2:]
        s1_copy(j, 0).start()
        s1_copy(j, 1).start()

        def near(q):
            part[slot, q] = quarter((x + jnp.where(q == 2, 3, q)) % 4)

        each(0, 3, near)

    def second(j):
        slot = j % HOLD
        mid = CHUNK // 2
        s1_wait(j, 0)
        s2[j, 0, :mid] = (part[slot, 1, :mid] + l1[j].astype(F32)).astype(BF16)
        s2[j, 0, mid:] = part[slot, 1, mid:].astype(BF16)
        s2_copy(j, 0).start()
        s1_wait(j, 1)
        s2[j, 1, :mid] = part[slot, 2, :mid].astype(BF16)
        s2[j, 1, mid:] = (part[slot, 2, mid:] + r1[j].astype(F32)).astype(BF16)
        s2_copy(j, 1).start()

    def s3_self(j, cc):
        return (2 * c + j // STRIPS == y) & (cc == c)

    def s3_copy(j, cc):
        return remote(
            s3.at[j, cc], r3.at[j % STRIPS, y], s3_s.at[j, cc], s3_r.at[j % STRIPS, y], dev(x, 2 * c + j // STRIPS, z, cc)
        )

    def third(j):
        slot = j % HOLD
        s2_wait(j, 0)
        s2_wait(j, 1)
        for cc in range(2):
            at = slice(cc * 2 * STRIP, (cc + 1) * 2 * STRIP)
            s3[j, cc] = part[slot, 0, at] + (l2[j, at].astype(F32) + r2[j, at].astype(F32))

            @pl.when(s3_self(j, cc))
            def _():
                pltpu.make_async_copy(s3.at[j, cc], r3.at[j % STRIPS, y], s3_r.at[j % STRIPS, y]).start()

            @pl.when(jnp.logical_not(s3_self(j, cc)))
            def _():
                s3_copy(j, cc).start()

    def z_send(n, zl, p):
        return remote(zs.at[n, zl, p], zr.at[n, z], z_s.at[n, zl, p], z_r.at[n, z], dev(x, y, 2 * p + zl, c))

    def fourth(n):
        for k in range(4):
            pltpu.make_async_copy(s3.at[0, 0], r3.at[n, k], s3_r.at[n, k]).wait()
        for zl in range(2):
            for h in range(2):
                at = slice(zl * STRIP + h * STRIP // 2, zl * STRIP + (h + 1) * STRIP // 2)
                total = (r3[n, 0, at] + r3[n, 1, at]) + (r3[n, 2, at] + r3[n, 3, at])
                zs[n, zl, 2 * h] = total[:, :128]
                zs[n, zl, 2 * h + 1] = total[:, 128:]

        def send(k):
            zl, p = k // 4, k % 4

            @pl.when(2 * p + zl == z)
            def _():
                pltpu.make_async_copy(zs.at[n, zl, p], zr.at[n, z], z_r.at[n, z]).start()

            @pl.when(2 * p + zl != z)
            def _():
                z_send(n, zl, p).start()

        each(0, 8, send)

    def a_copy(m, t):
        to = ((zhi + t) % 4) * 4 + x
        return remote(fb.at[m], ar.at[m, x, zhi], a_s.at[m, t], a_r.at[m, t], (to, me))

    def a_wait(m, t):
        remote(fb.at[m], ar.at[m, x, (zhi + 4 - t) % 4], a_s.at[m, t], a_r.at[m, t], sib).wait_recv()

    def b_copy(m, t):
        to = zhi * 4 + (x + t) % 4
        return remote(ar.at[m, x], ar.at[m, x], b_s.at[m, t], b_r.at[m, t], (to, me))

    def b_wait(m, t):
        src = (x + 4 - t) % 4
        remote(ar.at[m, src], ar.at[m, src], b_s.at[m, t], b_r.at[m, t], sib).wait_recv()

    def fifth(m):
        for e in range(2):
            n = 2 * m + e

            def wait(k):
                pltpu.make_async_copy(zs.at[0, 0, 0], zr.at[n, k], z_r.at[n, k]).wait()

            each(0, 8, wait)
        totals = []
        for e in range(2):
            total = zr[2 * m + e, 0]
            for k in range(1, 8):
                total = total + zr[2 * m + e, k]
            totals.append(total * FACTOR)
        both = jnp.concatenate(totals, axis=0).astype(BF16)
        fb[m] = both
        ar[m, x, zhi] = both
        each(1, 4, lambda t: a_copy(m, t).start())

    def sixth(m):
        each(1, 4, lambda t: a_wait(m, t))
        each(1, 4, lambda t: b_copy(m, t).start())

    first = STRIPS * (y % 2)

    def step(i):
        pl.when(i < CHUNKS)(lambda: matmul(i))
        pl.when((i >= 2) & (i < CHUNKS + 2))(lambda: second(i - 2))
        pl.when((i >= 4) & (i < CHUNKS + 4))(lambda: third(i - 4))
        n = i - 6 - first
        pl.when((n >= 0) & (n < STRIPS))(lambda: fourth(n))
        n = i - 8 - first
        pl.when((n >= 0) & (n < STRIPS) & (n % 2 == 1))(lambda: fifth(n // 2))
        n = i - 10 - first
        pl.when((n >= 0) & (n < STRIPS) & (n % 2 == 1))(lambda: sixth(n // 2))

        tasks = {
            0: [lambda: w_near(0, 0), lambda: w_near(1, 0), lambda: w_other(0, 0), lambda: w_other(0, 1), lambda: hidden_other(3)],
            1: [lambda: hidden_other(4), lambda: hidden_other(5), lambda: each(STRIPS, CHUNKS, lambda j: h_copy(j).start())],
            2: [lambda: w_near(0, 1), lambda: w_near(1, 1), lambda: delta(0)],
            3: [lambda: hidden_own(3), lambda: hidden_own(4), lambda: hidden_own(5)],
            4: [lambda: w_far(0), lambda: w_far(1), lambda: w_other(3, 0), lambda: w_other(1, 1)],
            6: [lambda: w_other(1, 0), lambda: w_other(3, 1)],
            7: [lambda: delta(1), lambda: w_other(2, 0), lambda: w_other(2, 1)],
            8: [lambda: delta(3)],
            9: [lambda: delta(2), gain_first],
            10: [finish],
            12: [gain_second],
        }
        for at, todo in tasks.items():
            def run(todo=todo):
                for task in todo:
                    task()

            pl.when(i == at)(run)

    each(0, CHUNKS + 10, step)

    gain_third()

    def place(m):
        each(1, 4, lambda t: b_wait(m, t))
        for xs in range(4):
            for p in range(4):
                both = ar[m, xs, p].astype(F32)
                lanes = slice(QUART * xs + 128 * (p % 2), QUART * xs + 128 * (p % 2) + 128)
                for e in range(2):
                    rows = ds((2 * m + e) * STRIP + STRIP // 2 * (p // 2), STRIP // 2, 8)
                    wg[rows, lanes] = both[e * STRIP // 2:(e + 1) * STRIP // 2]

    each(0, STRIPS // 2, place)

    def sent(t):
        gain_copy(t).wait_send()
        g1_copy(t).wait_send()
        g2_copy(t).wait_send()

    each(1, 16, sent)
    u_copy.wait_send()
    each(0, CHUNKS, lambda j: h_copy(j).wait_send())
    for way in range(2):
        for h in range(2):
            y_own(way, h).wait_send()
        y_pass(way).wait_send()
    for d in range(4):
        for h in range(2):
            z_half(d, h).wait_send()
            for k in range(2):
                c_half(d, h, k).wait_send()

    def sums_sent(j):
        for h in range(2):
            s1_copy(j, h).wait_send()
            s2_copy(j, h).wait_send()
            pl.when(jnp.logical_not(s3_self(j, h)))(lambda h=h: s3_copy(j, h).wait_send())

    each(0, CHUNKS, sums_sent)

    def z_sent(k):
        n, zl, p = k // 8, (k // 4) % 2, k % 4
        pl.when(2 * p + zl != z)(lambda: z_send(n, zl, p).wait_send())

    each(0, 8 * STRIPS, z_sent)

    def replicas_sent(m):
        def one(t):
            a_copy(m, t).wait_send()
            b_copy(m, t).wait_send()

        each(1, 4, one)

    each(0, STRIPS // 2, replicas_sent)


def local(inputs, gain, weight, upstream):
    vmem = pltpu.VMEM
    dma = pltpu.SemaphoreType.DMA
    anywhere = pl.BlockSpec(memory_space=pl.ANY)
    whole = pl.BlockSpec(memory_space=pltpu.VMEM)
    input_grad, weight_grad, gain_grad = pl.pallas_call(
        kernel,
        out_shape=(
            vmem((TOK, D), BF16),
            vmem((ROWS, COLS), F32),
            vmem((ROWS,), F32),
        ),
        in_specs=[anywhere, whole, anywhere, anywhere],
        out_specs=(whole, whole, whole),
        scratch_shapes=[
            vmem((TOK, D), BF16),
            vmem((D, COLS), BF16),
            vmem((TOK, D), F32),
            vmem((HALF, 2 * TOK), BF16),
            vmem((HALF, TOK), BF16),
            vmem((2 * TOK, COLS), BF16),
            vmem((TOK, 128), F32),
            vmem((TOK, 128), F32),
            vmem((1, PAD), F32),
            vmem((1, PAD), F32),
            vmem((16, 1, 512), F32),
            vmem((16, 1, 512), F32),
            vmem((16, 1, 512), F32),
            vmem((1, 512), F32),
            vmem((1, 512), F32),
            vmem((HOLD, 3, CHUNK, QUART), F32),
            vmem((CHUNKS, 2, CHUNK // 2, QUART), BF16),
            vmem((CHUNKS, CHUNK // 2, QUART), BF16),
            vmem((CHUNKS, CHUNK // 2, QUART), BF16),
            vmem((CHUNKS, 2, CHUNK, QUART), BF16),
            vmem((CHUNKS, CHUNK, QUART), BF16),
            vmem((CHUNKS, CHUNK, QUART), BF16),
            vmem((CHUNKS, 2, CHUNK // 2, QUART), F32),
            vmem((STRIPS, 4, CHUNK // 2, QUART), F32),
            vmem((STRIPS, 2, 4, STRIP // 2, 128), F32),
            vmem((STRIPS, 8, STRIP // 2, 128), F32),
            vmem((STRIPS // 2, STRIP, 128), BF16),
            vmem((STRIPS // 2, 4, 4, STRIP, 128), BF16),
            dma((8,)), dma, dma,
            dma((16,)), dma((16,)), dma((16,)), dma((16,)), dma((16,)), dma((16,)),
            dma, dma, dma((CHUNKS,)), dma((CHUNKS,)),
            dma((3, 2)), dma((3, 2)), dma((4, 2)), dma((4, 2)), dma((4, 2, 2)), dma((4, 2, 2)),
            dma((CHUNKS, 2)), dma((CHUNKS, 2)), dma((CHUNKS, 2)), dma((CHUNKS, 2)), dma((CHUNKS, 2)), dma((STRIPS, 4)),
            dma((STRIPS, 2, 4)), dma((STRIPS, 8)),
            dma((STRIPS // 2, 4)), dma((STRIPS // 2, 4)), dma((STRIPS // 2, 4)), dma((STRIPS // 2, 4)),
        ],
        compiler_params=pltpu.CompilerParams(
            collective_id=0, has_side_effects=True, vmem_limit_bytes=54 << 20
        ),
        name="backward",
    )(inputs, gain, weight, upstream)
    return input_grad, weight_grad, gain_grad


def solution(mesh):
    return jax.shard_map(
        local,
        mesh=mesh,
        in_specs=(
            P(("rep", "shard"), None),
            P("shard"),
            P("shard", None),
            P(("rep", "shard"), None),
        ),
        out_specs=(P(("rep", "shard"), None), P("shard", None), P("shard")),
        check_vma=False,
    )
```

```python
import math

import jax
import jax.numpy as jnp
from jax import lax
from jax.experimental import pallas as pl
from jax.experimental.pallas import tpu as pltpu
from jax.sharding import PartitionSpec as P

MESH = pl.DeviceIdType.MESH
F32 = jnp.float32
BF16 = jnp.bfloat16
TOK = 512
D = 4608
COLS = 1024
ROWS = 288
HALF = D // 2
SUB = 384
QUART = COLS // 4
PAD = D + 128
STRIP = 48
CHUNK = 4 * STRIP
CHUNKS = HALF // CHUNK
STRIPS = ROWS // STRIP
HOLD = 5
FACTOR = 1.0 / math.sqrt(131072)


def ds(start, size, unit):
    return pl.ds(pl.multiple_of(start, unit), size)


def remote(src, dst, send, recv, device):
    return pltpu.make_async_remote_copy(
        src_ref=src, dst_ref=dst, send_sem=send, recv_sem=recv, device_id=device, device_id_type=MESH
    )


def each(first, last, step):
    def body(t, carry):
        step(t)
        return carry

    lax.fori_loop(first, last, body, 0)


def kernel(
    x_hbm, gain, w_hbm, u_hbm,
    ig, wg, gg,
    xv, wv, sv, ht, hs, ups, inv, rd, gfull, gsum, gbuf, gone, gtwo, gmine, win,
    part, s1, l1, r1, s2, l2, r2, s3, r3, zs, zr, fb, ar,
    ld_x, ld_u, ld_w,
    gb_s, gb_r, g1_s, g1_r, g2_s, g2_r,
    u_s, u_r, h_s, h_r,
    wy_s, wy_r, wz_s, wz_r, wc_s, wc_r,
    s1_s, s1_r, s2_s, s2_r, s3_s, s3_r, z_s, z_r, a_s, a_r, b_s, b_r,
):
    rep = lax.axis_index("rep")
    me = lax.axis_index("shard")
    x, zhi = rep % 4, rep // 4
    y, zlo, c = me // 4, (me // 2) % 2, me % 2
    z = zhi * 2 + zlo

    def dev(xx, yy, zz, cc):
        return ((zz // 2) * 4 + xx, (yy * 2 + zz % 2) * 2 + cc)

    sib = (rep, me + 1 - 2 * c)
    right, left = dev((x + 1) % 4, y, z, c), dev((x + 3) % 4, y, z, c)
    up, down = dev(x, y, (z + 1) % 8, c), dev(x, y, (z + 7) % 8, c)

    row = jnp.concatenate([gain[...].astype(F32).reshape(1, ROWS), jnp.zeros((1, 512 - ROWS), F32)], axis=1)
    win[...] = pltpu.roll(jnp.broadcast_to(row, (8, 512)), (32 * me) % 128, 1)[:1]

    def load_x(k):
        rows = ds(k * 64, 64, 64)
        return pltpu.make_async_copy(x_hbm.at[rows, :], xv.at[rows, :], ld_x.at[k])

    each(0, 8, lambda k: load_x(k).start())
    own_tok = ds(c * TOK, TOK, TOK)
    load_u = pltpu.make_async_copy(u_hbm, ups.at[own_tok, :], ld_u)
    load_u.start()
    own_rows = ds(me * ROWS, ROWS, 32)
    load_w = pltpu.make_async_copy(w_hbm, wv.at[own_rows, :], ld_w)
    load_w.start()

    barrier = pltpu.get_barrier_semaphore()

    def hello(device):
        pl.semaphore_signal(barrier, inc=1, device_id=device, device_id_type=MESH)

    each(1, 16, lambda t: hello((rep, (me + t) % 16)))
    each(1, 16, lambda t: hello(((rep + t) % 16, me)))
    each(1, 4, lambda t: hello((((zhi + t) % 4) * 4 + x, (y * 2 + 1 - zlo) * 2 + c)))
    pl.semaphore_wait(barrier, 33)

    def gain_copy(t):
        return remote(win, gbuf.at[me], gb_s.at[t], gb_r.at[t], (rep, (me + t) % 16))

    each(1, 16, lambda t: gain_copy(t).start())
    gbuf[me] = win[...]
    u_copy = remote(u_hbm, ups.at[own_tok, :], u_s, u_r, sib)
    u_copy.start()

    def w_half(d, zl, cc, h):
        return ds(((((y + d) % 4) * 2 + zl) * 2 + cc) * ROWS + h * 144, 144, 16)

    def y_own(way, h):
        rows = w_half(0, zlo, c, h)
        to = dev(x, (y + (1 if way == 0 else 3)) % 4, z, c)
        return remote(wv.at[rows, :], wv.at[rows, :], wy_s.at[way, h], wy_r.at[way, h], to)

    def y_pass(way):
        rows = w_half(3 if way == 0 else 1, zlo, c, way)
        to = dev(x, (y + (1 if way == 0 else 3)) % 4, z, c)
        return remote(wv.at[rows, :], wv.at[rows, :], wy_s.at[2, way], wy_r.at[2, way], to)

    def z_half(d, h):
        rows = w_half(d, zlo, c, h)
        return remote(wv.at[rows, :], wv.at[rows, :], wz_s.at[d, h], wz_r.at[d, h], up if h == 0 else down)

    def c_half(d, h, k):
        rows = w_half(d, zlo if k == 0 else 1 - zlo, c, h)
        return remote(wv.at[rows, :], wv.at[rows, :], wc_s.at[d, h, k], wc_r.at[d, h, k], sib)

    def arrive(rows, sem):
        remote(wv.at[rows, :], wv.at[rows, :], wc_s.at[0, 0, 0], sem, sib).wait_recv()

    def w_have(d, h):
        z_half(d, h).start()
        c_half(d, h, 0).start()

    def w_near(h, k):
        way = h if k == 0 else 1 - h
        d = 3 if way == 0 else 1
        arrive(w_half(d, zlo, c, h), wy_r.at[way, h])
        if k == 0:
            y_pass(way).start()
        w_have(d, h)

    def w_far(h):
        arrive(w_half(2, zlo, c, h), wy_r.at[2, h])
        w_have(2, h)

    def w_other(d, h):
        arrive(w_half(d, 1 - zlo, c, h), wz_r.at[d, h])
        c_half(d, h, 1).start()

    load_w.wait()
    for way in (0, 1):
        y_own(way, way).start()
        w_have(0, way)
    for way in (0, 1):
        y_own(way, 1 - way).start()

    def norm_block(k):
        load_x(k).wait()
        rows = ds(k * 64, 64, 64)
        total = jnp.zeros((64, 128), F32)
        for j in range(D // 512):
            v = xv[rows, j * 512:(j + 1) * 512].astype(F32)
            v = v * v
            total = total + ((v[:, :128] + v[:, 128:256]) + (v[:, 256:384] + v[:, 384:]))
        mean = jnp.sum(total, axis=-1, keepdims=True) * (1.0 / D)
        inv[rows, :] = jnp.broadcast_to(lax.rsqrt(mean + 1e-06), (64, 128))

    each(0, 8, norm_block)

    def gain_wait(t):
        remote(win, gbuf.at[(me + 16 - t) % 16], gb_s.at[t], gb_r.at[t], sib).wait_recv()

    each(1, 16, gain_wait)
    gfull[...] = jnp.ones((1, PAD), F32)
    for s in range(16):
        at = (ROWS * s) // 128 * 128
        gfull[:, at:at + 512] = gfull[:, at:at + 512] + gbuf[s]

    def inv3(rows):
        iv = inv[rows, :]
        return jnp.concatenate([iv, iv, iv], axis=1)

    def hidden_block(j, at_feature, out, at_lane):
        feats = ds(at_feature + j * SUB, SUB, 128)
        scale = gfull[:, feats]

        def tokens(k):
            rows = ds(k * 128, 128, 128)
            v = xv[rows, feats].astype(F32) * inv3(rows)
            v = (v * scale).astype(BF16).T
            for e in range(SUB // STRIP):
                strip = j * (SUB // STRIP) + e
                shard, nth = strip // STRIPS, strip % STRIPS
                to = ((shard // 4) * STRIPS + nth) * CHUNK + ((shard % 2) * 2 + (shard // 2) % 2) * STRIP
                out[ds(to, STRIP, 16), ds(at_lane + k * 128, 128, 128)] = v[e * STRIP:(e + 1) * STRIP]

        each(0, 4, tokens)

    def h_copy(j):
        rows = ds(j * CHUNK, CHUNK, CHUNK)
        return remote(hs.at[rows, :], ht.at[rows, own_tok], h_s.at[j], h_r.at[j], sib)

    def h_wait(j):
        rows = ds(j * CHUNK, CHUNK, CHUNK)
        remote(hs.at[rows, :], ht.at[rows, ds((1 - c) * TOK, TOK, TOK)], h_s.at[j], h_r.at[j], sib).wait_recv()

    def hidden_other(j):
        hidden_block(j, (1 - c) * HALF, hs, 0)

    def hidden_own(j):
        hidden_block(j, c * HALF, ht, c * TOK)

    odd = y % 2
    early, late = 3 * odd, 3 * (1 - odd)

    def chunk_of(i):
        return ((i // STRIPS + odd) % 2) * STRIPS + i % STRIPS

    each(0, 3, lambda j: hidden_other(early + j))
    each(0, STRIPS, lambda j: h_copy(chunk_of(j)).start())
    each(0, 3, lambda j: hidden_own(early + j))
    load_u.wait()
    remote(u_hbm, ups.at[ds((1 - c) * TOK, TOK, TOK), :], u_s, u_r, sib).wait_recv()

    rd[...] = jnp.zeros_like(rd)
    gsum[...] = jnp.zeros_like(gsum)

    def projection(d):
        for h in range(2):
            for k in range(2):
                arrive(w_half(d, zlo if k == 0 else 1 - zlo, 1 - c, h), wc_r.at[d, h, k])

    def delta(b):
        e = b // 3
        d = jnp.where(e == 2, 3, jnp.where(e == 3, 2, e))
        at = ((y + d) % 4) * 1152 + (b % 3) * SUB
        feats = ds(at, SUB, 128)
        sv[:, feats] = lax.dot_general(
            ups[own_tok, :], wv[ds(at, SUB, 32), :], (((1,), (1,)), ((), ())), preferred_element_type=F32
        )
        scale = gfull[:, feats]

        def tokens(k, col):
            rows = ds(k * 64, 64, 64)
            dl = sv[rows, feats]
            nm = xv[rows, feats].astype(F32) * inv3(rows)
            dn = dl * nm
            sn = dn * scale
            sv[rows, feats] = dl * scale
            rd[rows, :] = rd[rows, :] + (sn[:, :128] + sn[:, 128:256] + sn[:, 256:])
            return col + jnp.sum(dn.reshape(8, 8, SUB), axis=0)

        col = lax.fori_loop(0, 8, tokens, jnp.zeros((8, SUB), F32))
        gsum[:, feats] = jnp.sum(col, axis=0, keepdims=True)

    def finish(first, last):
        def block(j):
            rows = ds(j * 64, 64, 64)
            m = jnp.sum(rd[rows, :], axis=-1, keepdims=True) * (1.0 / D)
            m = jnp.broadcast_to(m, (64, 128))
            m = jnp.concatenate([m, m, m], axis=1)

            def part_of(k):
                feats = ds(k * SUB, SUB, 128)
                iv = inv3(rows)
                nm = xv[rows, feats].astype(F32) * iv
                ig[rows, feats] = (iv * (sv[rows, feats] - nm * m)).astype(BF16)

            each(0, 12, part_of)

        each(first, last, block)

    def gain_window(s):
        return ds(s * ROWS - (32 * s) % 128, 512, 128)

    def g1_copy(t):
        to = (me + t) % 16
        return remote(gsum.at[:, gain_window(to)], gone.at[me], g1_s.at[t], g1_r.at[t], (rep, to))

    def g1_wait(t):
        remote(gmine, gone.at[(me + 16 - t) % 16], g1_s.at[t], g1_r.at[t], sib).wait_recv()

    def g2_copy(t):
        return remote(gmine, gtwo.at[rep], g2_s.at[t], g2_r.at[t], ((rep + t) % 16, me))

    def g2_wait(t):
        remote(gmine, gtwo.at[(rep + 16 - t) % 16], g2_s.at[t], g2_r.at[t], sib).wait_recv()

    def gain_first():
        each(1, 16, lambda t: g1_copy(t).start())
        gone[me] = gsum[:, gain_window(me)]

    def gain_second():
        each(1, 16, g1_wait)
        total = gone[0]
        for s in range(1, 16):
            total = total + gone[s]
        gmine[...] = total
        gtwo[rep] = total
        each(1, 16, lambda t: g2_copy(t).start())

    def gain_third():
        each(1, 16, g2_wait)
        total = gtwo[0]
        for s in range(1, 16):
            total = total + gtwo[s]
        total = jnp.broadcast_to(total * FACTOR, (8, 512))
        gg[...] = pltpu.roll(total, (512 - (32 * me) % 128) % 512, 1)[0, :ROWS]

    def s1_copy(j, h):
        return remote(s1.at[j, h], (l1 if h == 0 else r1).at[j], s1_s.at[j, h], s1_r.at[j, h], right if h == 0 else left)

    def s1_wait(j, h):
        remote(s1.at[j, h], (l1 if h == 0 else r1).at[j], s1_s.at[j, h], s1_r.at[j, h], left).wait_recv()

    def s2_copy(j, h):
        return remote(s2.at[j, h], (l2 if h == 0 else r2).at[j], s2_s.at[j, h], s2_r.at[j, h], right if h == 0 else left)

    def s2_wait(j, h):
        remote(s2.at[j, h], (l2 if h == 0 else r2).at[j], s2_s.at[j, h], s2_r.at[j, h], left).wait_recv()

    def matmul(j):
        h_wait(chunk_of(j))
        slot = j % HOLD
        rows = ds(chunk_of(j) * CHUNK, CHUNK, CHUNK)

        def quarter(q):
            return jnp.dot(ht[rows, :], ups[:, ds(q * QUART, QUART, 128)], preferred_element_type=F32)

        far = quarter((x + 2) % 4).astype(BF16)
        s1[j, 0] = far[:CHUNK // 2]
        s1[j, 1] = far[CHUNK // 2:]
        s1_copy(j, 0).start()
        s1_copy(j, 1).start()

        def near(q):
            part[slot, q] = quarter((x + jnp.where(q == 2, 3, q)) % 4)

        each(0, 3, near)

    def second(j):
        slot = j % HOLD
        mid = CHUNK // 2
        s1_wait(j, 0)
        s2[j, 0, :mid] = (part[slot, 1, :mid] + l1[j].astype(F32)).astype(BF16)
        s2[j, 0, mid:] = part[slot, 1, mid:].astype(BF16)
        s2_copy(j, 0).start()
        s1_wait(j, 1)
        s2[j, 1, :mid] = part[slot, 2, :mid].astype(BF16)
        s2[j, 1, mid:] = (part[slot, 2, mid:] + r1[j].astype(F32)).astype(BF16)
        s2_copy(j, 1).start()

    def s3_to(j):
        return 2 * c + (j // STRIPS + odd) % 2

    def s3_self(j, cc):
        return (s3_to(j) == y) & (cc == c)

    def s3_copy(j, cc):
        return remote(
            s3.at[j, cc], r3.at[j % STRIPS, y], s3_s.at[j, cc], s3_r.at[j % STRIPS, y], dev(x, s3_to(j), z, cc)
        )

    def third(j):
        slot = j % HOLD
        s2_wait(j, 0)
        s2_wait(j, 1)
        for cc in range(2):
            at = slice(cc * 2 * STRIP, (cc + 1) * 2 * STRIP)
            s3[j, cc] = part[slot, 0, at] + (l2[j, at].astype(F32) + r2[j, at].astype(F32))

            @pl.when(s3_self(j, cc))
            def _():
                pltpu.make_async_copy(s3.at[j, cc], r3.at[j % STRIPS, y], s3_r.at[j % STRIPS, y]).start()

            @pl.when(jnp.logical_not(s3_self(j, cc)))
            def _():
                s3_copy(j, cc).start()

    def z_send(n, zl, p):
        return remote(zs.at[n, zl, p], zr.at[n, z], z_s.at[n, zl, p], z_r.at[n, z], dev(x, y, 2 * p + zl, c))

    def fourth(n):
        for k in range(4):
            pltpu.make_async_copy(s3.at[0, 0], r3.at[n, k], s3_r.at[n, k]).wait()
        for zl in range(2):
            for h in range(2):
                at = slice(zl * STRIP + h * STRIP // 2, zl * STRIP + (h + 1) * STRIP // 2)
                total = (r3[n, 0, at] + r3[n, 1, at]) + (r3[n, 2, at] + r3[n, 3, at])
                zs[n, zl, 2 * h] = total[:, :128]
                zs[n, zl, 2 * h + 1] = total[:, 128:]

        def send(k):
            zl, p = k // 4, k % 4

            @pl.when(2 * p + zl == z)
            def _():
                pltpu.make_async_copy(zs.at[n, zl, p], zr.at[n, z], z_r.at[n, z]).start()

            @pl.when(2 * p + zl != z)
            def _():
                z_send(n, zl, p).start()

        each(0, 8, send)

    def a_copy(m, t):
        to = ((zhi + t) % 4) * 4 + x
        return remote(fb.at[m], ar.at[m, x, zhi], a_s.at[m, t], a_r.at[m, t], (to, me))

    def a_wait(m, t):
        remote(fb.at[m], ar.at[m, x, (zhi + 4 - t) % 4], a_s.at[m, t], a_r.at[m, t], sib).wait_recv()

    def b_copy(m, t):
        to = zhi * 4 + (x + t) % 4
        return remote(ar.at[m, x], ar.at[m, x], b_s.at[m, t], b_r.at[m, t], (to, me))

    def b_wait(m, t):
        src = (x + 4 - t) % 4
        remote(ar.at[m, src], ar.at[m, src], b_s.at[m, t], b_r.at[m, t], sib).wait_recv()

    def fifth(m):
        for e in range(2):
            n = 2 * m + e

            def wait(k):
                pltpu.make_async_copy(zs.at[0, 0, 0], zr.at[n, k], z_r.at[n, k]).wait()

            each(0, 8, wait)
        totals = []
        for e in range(2):
            total = zr[2 * m + e, 0]
            for k in range(1, 8):
                total = total + zr[2 * m + e, k]
            totals.append(total * FACTOR)
        both = jnp.concatenate(totals, axis=0).astype(BF16)
        fb[m] = both
        ar[m, x, zhi] = both
        each(1, 4, lambda t: a_copy(m, t).start())

    def sixth(m):
        each(1, 4, lambda t: a_wait(m, t))
        each(1, 4, lambda t: b_copy(m, t).start())

    def place(m):
        each(1, 4, lambda t: b_wait(m, t))
        for xs in range(4):
            for p in range(4):
                both = ar[m, xs, p].astype(F32)
                lanes = slice(QUART * xs + 128 * (p % 2), QUART * xs + 128 * (p % 2) + 128)
                for e in range(2):
                    rows = ds((2 * m + e) * STRIP + STRIP // 2 * (p // 2), STRIP // 2, 8)
                    wg[rows, lanes] = both[e * STRIP // 2:(e + 1) * STRIP // 2]

    def step(i):
        pl.when(i < CHUNKS)(lambda: matmul(i))
        pl.when((i >= 2) & (i < CHUNKS + 2))(lambda: second(i - 2))
        pl.when((i >= 4) & (i < CHUNKS + 4))(lambda: third(i - 4))
        n = i - 6 - STRIPS
        pl.when((n >= 0) & (n < STRIPS))(lambda: fourth(n))
        n = i - 8 - STRIPS
        pl.when((n >= 0) & (n < STRIPS) & (n % 2 == 1))(lambda: fifth(n // 2))
        n = i - 10 - STRIPS
        pl.when((n >= 0) & (n < STRIPS) & (n % 2 == 1))(lambda: sixth(n // 2))

        tasks = {
            0: [lambda: each(0, 2, lambda j: hidden_other(late + j))],
            1: [lambda: hidden_other(late + 2), lambda: each(STRIPS, CHUNKS, lambda j: h_copy(chunk_of(j)).start()),
                lambda: w_near(0, 0), lambda: w_near(1, 0), lambda: w_other(0, 0), lambda: w_other(0, 1),
                lambda: hidden_own(late)],
            2: [lambda: hidden_own(late + 1)],
            3: [lambda: w_near(0, 1), lambda: w_near(1, 1), lambda: hidden_own(late + 2)],
            4: [lambda: projection(0)],
            5: [lambda: w_far(0), lambda: w_far(1), lambda: w_other(3, 0), lambda: w_other(1, 1)],
            7: [lambda: w_other(1, 0), lambda: w_other(3, 1)],
            8: [lambda: projection(1)],
            9: [lambda: w_other(2, 0), lambda: w_other(2, 1)],
            11: [lambda: projection(3)],
            14: [lambda: projection(2)],
            17: [gain_first],
            19: [gain_second],
            20: [lambda: place(0)],
            21: [lambda: place(1)],
        }
        for at, todo in tasks.items():
            def run(todo=todo):
                for task in todo:
                    task()

            pl.when(i == at)(run)

        pl.when(((i >= 4) & (i < 7)) | ((i >= 8) & (i < 17)))(lambda: delta(jnp.where(i < 7, i - 4, i - 5)))
        pl.when((i >= 17) & (i < 21))(lambda: finish(2 * (i - 17), 2 * (i - 17) + 2))

    each(0, CHUNKS + 10, step)

    gain_third()
    place(2)

    def sent(t):
        gain_copy(t).wait_send()
        g1_copy(t).wait_send()
        g2_copy(t).wait_send()

    each(1, 16, sent)
    u_copy.wait_send()
    each(0, CHUNKS, lambda j: h_copy(j).wait_send())
    for way in range(2):
        for h in range(2):
            y_own(way, h).wait_send()
        y_pass(way).wait_send()
    for d in range(4):
        for h in range(2):
            z_half(d, h).wait_send()
            for k in range(2):
                c_half(d, h, k).wait_send()

    def sums_sent(j):
        for h in range(2):
            s1_copy(j, h).wait_send()
            s2_copy(j, h).wait_send()
            pl.when(jnp.logical_not(s3_self(j, h)))(lambda h=h: s3_copy(j, h).wait_send())

    each(0, CHUNKS, sums_sent)

    def z_sent(k):
        n, zl, p = k // 8, (k // 4) % 2, k % 4
        pl.when(2 * p + zl != z)(lambda: z_send(n, zl, p).wait_send())

    each(0, 8 * STRIPS, z_sent)

    def replicas_sent(m):
        def one(t):
            a_copy(m, t).wait_send()
            b_copy(m, t).wait_send()

        each(1, 4, one)

    each(0, STRIPS // 2, replicas_sent)


def hand_out(ig, wg, gg, ig_hbm, wg_hbm, gg_hbm, sems):
    copies = [pltpu.make_async_copy(ig.at[pl.ds(k * 64, 64)], ig_hbm.at[pl.ds(k * 64, 64)], sems.at[k]) for k in range(8)]
    copies += [pltpu.make_async_copy(wg, wg_hbm, sems.at[8]), pltpu.make_async_copy(gg, gg_hbm, sems.at[9])]
    for copy in copies:
        copy.start()
    for copy in copies:
        copy.wait()


def local(inputs, gain, weight, upstream):
    vmem = pltpu.VMEM
    dma = pltpu.SemaphoreType.DMA
    anywhere = pl.BlockSpec(memory_space=pl.ANY)
    whole = pl.BlockSpec(memory_space=pltpu.VMEM)
    input_grad, weight_grad, gain_grad = pl.pallas_call(
        kernel,
        out_shape=(
            vmem((TOK, D), BF16),
            vmem((ROWS, COLS), F32),
            vmem((ROWS,), F32),
        ),
        in_specs=[anywhere, whole, anywhere, anywhere],
        out_specs=(whole, whole, whole),
        scratch_shapes=[
            vmem((TOK, D), BF16),
            vmem((D, COLS), BF16),
            vmem((TOK, D), F32),
            vmem((HALF, 2 * TOK), BF16),
            vmem((HALF, TOK), BF16),
            vmem((2 * TOK, COLS), BF16),
            vmem((TOK, 128), F32),
            vmem((TOK, 128), F32),
            vmem((1, PAD), F32),
            vmem((1, PAD), F32),
            vmem((16, 1, 512), F32),
            vmem((16, 1, 512), F32),
            vmem((16, 1, 512), F32),
            vmem((1, 512), F32),
            vmem((1, 512), F32),
            vmem((HOLD, 3, CHUNK, QUART), F32),
            vmem((CHUNKS, 2, CHUNK // 2, QUART), BF16),
            vmem((CHUNKS, CHUNK // 2, QUART), BF16),
            vmem((CHUNKS, CHUNK // 2, QUART), BF16),
            vmem((CHUNKS, 2, CHUNK, QUART), BF16),
            vmem((CHUNKS, CHUNK, QUART), BF16),
            vmem((CHUNKS, CHUNK, QUART), BF16),
            vmem((CHUNKS, 2, CHUNK // 2, QUART), F32),
            vmem((STRIPS, 4, CHUNK // 2, QUART), F32),
            vmem((STRIPS, 2, 4, STRIP // 2, 128), F32),
            vmem((STRIPS, 8, STRIP // 2, 128), F32),
            vmem((STRIPS // 2, STRIP, 128), BF16),
            vmem((STRIPS // 2, 4, 4, STRIP, 128), BF16),
            dma((8,)), dma, dma,
            dma((16,)), dma((16,)), dma((16,)), dma((16,)), dma((16,)), dma((16,)),
            dma, dma, dma((CHUNKS,)), dma((CHUNKS,)),
            dma((3, 2)), dma((3, 2)), dma((4, 2)), dma((4, 2)), dma((4, 2, 2)), dma((4, 2, 2)),
            dma((CHUNKS, 2)), dma((CHUNKS, 2)), dma((CHUNKS, 2)), dma((CHUNKS, 2)), dma((CHUNKS, 2)), dma((STRIPS, 4)),
            dma((STRIPS, 2, 4)), dma((STRIPS, 8)),
            dma((STRIPS // 2, 4)), dma((STRIPS // 2, 4)), dma((STRIPS // 2, 4)), dma((STRIPS // 2, 4)),
        ],
        compiler_params=pltpu.CompilerParams(
            collective_id=0, has_side_effects=True, vmem_limit_bytes=54 << 20
        ),
        name="backward",
    )(inputs, gain, weight, upstream)
    held = [pltpu.with_memory_space_constraint(a, pltpu.VMEM) for a in (input_grad, weight_grad, gain_grad)]
    return pl.pallas_call(
        hand_out,
        out_shape=tuple(jax.ShapeDtypeStruct(a.shape, a.dtype) for a in held),
        in_specs=[whole] * 3,
        out_specs=(anywhere,) * 3,
        scratch_shapes=[dma((10,))],
        compiler_params=pltpu.CompilerParams(vmem_limit_bytes=1 << 20),
        name="hand_out",
    )(*held)


def solution(mesh):
    return jax.shard_map(
        local,
        mesh=mesh,
        in_specs=(
            P(("rep", "shard"), None),
            P("shard"),
            P("shard", None),
            P(("rep", "shard"), None),
        ),
        out_specs=(P(("rep", "shard"), None), P("shard", None), P("shard")),
        check_vma=False,
    )
```

```python
import math

import jax
import jax.numpy as jnp
from jax import lax
from jax.experimental import pallas as pl
from jax.experimental.pallas import tpu as pltpu
from jax.sharding import PartitionSpec as P

MESH = pl.DeviceIdType.MESH
F32 = jnp.float32
BF16 = jnp.bfloat16
TOK = 512
D = 4608
COLS = 1024
ROWS = 288
HALF = D // 2
SUB = 384
QUART = COLS // 4
PAD = D + 128
STRIP = 48
CHUNK = 4 * STRIP
CHUNKS = HALF // CHUNK
STRIPS = ROWS // STRIP
HOLD = 5
FACTOR = 1.0 / math.sqrt(131072)


def ds(start, size, unit):
    return pl.ds(pl.multiple_of(start, unit), size)


def remote(src, dst, send, recv, device):
    return pltpu.make_async_remote_copy(
        src_ref=src, dst_ref=dst, send_sem=send, recv_sem=recv, device_id=device, device_id_type=MESH
    )


def each(first, last, step):
    def body(t, carry):
        step(t)
        return carry

    lax.fori_loop(first, last, body, 0)


def kernel(
    x_hbm, gain_hbm, w_hbm, u_hbm,
    ig, wg, gg,
    xv, wv, sv, ht, hs, ups, inv, rd, gfull, gsum, gbuf, gone, gtwo, gmine, gpart, win, gain,
    part, s1, l1, r1, s2, l2, r2, s3, r3, zs, zr, fb, ar,
    ld_g, ld_x, ld_u, ld_w,
    gb_s, gb_r, g1_s, g1_r, g2_s, g2_r,
    u_s, u_r, h_s, h_r,
    wy_s, wy_r, wz_s, wz_r, wc_s, wc_r,
    s1_s, s1_r, s2_s, s2_r, s3_s, s3_r, z_s, z_r, a_s, a_r, b_s, b_r,
):
    rep = lax.axis_index("rep")
    me = lax.axis_index("shard")
    x, zhi = rep % 4, rep // 4
    y, zlo, c = me // 4, (me // 2) % 2, me % 2
    z = zhi * 2 + zlo

    def dev(xx, yy, zz, cc):
        return ((zz // 2) * 4 + xx, (yy * 2 + zz % 2) * 2 + cc)

    sib = (rep, me + 1 - 2 * c)
    right, left = dev((x + 1) % 4, y, z, c), dev((x + 3) % 4, y, z, c)
    up, down = dev(x, y, (z + 1) % 8, c), dev(x, y, (z + 7) % 8, c)

    barrier = pltpu.get_barrier_semaphore()

    def hello(device):
        pl.semaphore_signal(barrier, inc=1, device_id=device, device_id_type=MESH)

    each(1, 16, lambda t: hello((rep, (me + t) % 16)))

    def hello_far(t):
        far = ((zhi + t) % 4) * 4 + x
        hello((far, me))
        hello((far, (y * 2 + 1 - zlo) * 2 + c))
        hello((zhi * 4 + (x + t) % 4, me))

    each(1, 4, hello_far)

    load_g = pltpu.make_async_copy(gain_hbm, gain, ld_g)
    load_g.start()

    def load_x(k):
        rows = ds(k * 64, 64, 64)
        return pltpu.make_async_copy(x_hbm.at[rows, :], xv.at[rows, :], ld_x.at[k])

    each(0, 8, lambda k: load_x(k).start())
    own_tok = ds(c * TOK, TOK, TOK)
    load_u = pltpu.make_async_copy(u_hbm, ups.at[own_tok, :], ld_u)
    load_u.start()
    own_rows = ds(me * ROWS, ROWS, 32)
    load_w = pltpu.make_async_copy(w_hbm, wv.at[own_rows, :], ld_w)
    load_w.start()

    load_g.wait()
    row = jnp.concatenate([gain[...].astype(F32).reshape(1, ROWS), jnp.zeros((1, 512 - ROWS), F32)], axis=1)
    win[...] = pltpu.roll(jnp.broadcast_to(row, (8, 512)), (32 * me) % 128, 1)[:1]

    pl.semaphore_wait(barrier, 24)

    def gain_copy(t):
        return remote(win, gbuf.at[me], gb_s.at[t], gb_r.at[t], (rep, (me + t) % 16))

    each(1, 16, lambda t: gain_copy(t).start())
    gbuf[me] = win[...]
    u_copy = remote(u_hbm, ups.at[own_tok, :], u_s, u_r, sib)
    u_copy.start()

    def w_half(d, zl, cc, h):
        return ds(((((y + d) % 4) * 2 + zl) * 2 + cc) * ROWS + h * 144, 144, 16)

    def y_own(way, h):
        rows = w_half(0, zlo, c, h)
        to = dev(x, (y + (1 if way == 0 else 3)) % 4, z, c)
        return remote(wv.at[rows, :], wv.at[rows, :], wy_s.at[way, h], wy_r.at[way, h], to)

    def y_pass(way):
        rows = w_half(3 if way == 0 else 1, zlo, c, way)
        to = dev(x, (y + (1 if way == 0 else 3)) % 4, z, c)
        return remote(wv.at[rows, :], wv.at[rows, :], wy_s.at[2, way], wy_r.at[2, way], to)

    def z_half(d, h):
        rows = w_half(d, zlo, c, h)
        return remote(wv.at[rows, :], wv.at[rows, :], wz_s.at[d, h], wz_r.at[d, h], up if h == 0 else down)

    def c_half(d, h, k):
        rows = w_half(d, zlo if k == 0 else 1 - zlo, c, h)
        return remote(wv.at[rows, :], wv.at[rows, :], wc_s.at[d, h, k], wc_r.at[d, h, k], sib)

    def arrive(rows, sem):
        remote(wv.at[rows, :], wv.at[rows, :], wc_s.at[0, 0, 0], sem, sib).wait_recv()

    def w_have(d, h):
        z_half(d, h).start()
        c_half(d, h, 0).start()

    def w_near(h, k):
        way = h if k == 0 else 1 - h
        d = 3 if way == 0 else 1
        arrive(w_half(d, zlo, c, h), wy_r.at[way, h])
        if k == 0:
            y_pass(way).start()
        w_have(d, h)

    def w_far(h):
        arrive(w_half(2, zlo, c, h), wy_r.at[2, h])
        w_have(2, h)

    def w_other(d, h):
        arrive(w_half(d, 1 - zlo, c, h), wz_r.at[d, h])
        c_half(d, h, 1).start()

    load_w.wait()
    for way in (0, 1):
        y_own(way, way).start()
        w_have(0, way)
    for way in (0, 1):
        y_own(way, 1 - way).start()

    def norm_block(k):
        load_x(k).wait()
        rows = ds(k * 64, 64, 64)
        total = jnp.zeros((64, 128), F32)
        for j in range(D // 512):
            v = xv[rows, j * 512:(j + 1) * 512].astype(F32)
            v = v * v
            total = total + ((v[:, :128] + v[:, 128:256]) + (v[:, 256:384] + v[:, 384:]))
        mean = jnp.sum(total, axis=-1, keepdims=True) * (1.0 / D)
        inv[rows, :] = jnp.broadcast_to(lax.rsqrt(mean + 1e-06), (64, 128))

    each(0, 8, norm_block)

    def gain_wait(t):
        remote(win, gbuf.at[(me + 16 - t) % 16], gb_s.at[t], gb_r.at[t], sib).wait_recv()

    each(1, 16, gain_wait)
    gfull[...] = jnp.ones((1, PAD), F32)
    for s in range(16):
        at = (ROWS * s) // 128 * 128
        gfull[:, at:at + 512] = gfull[:, at:at + 512] + gbuf[s]

    def inv3(rows):
        iv = inv[rows, :]
        return jnp.concatenate([iv, iv, iv], axis=1)

    def hidden_block(j, at_feature, out, at_lane):
        feats = ds(at_feature + j * SUB, SUB, 128)
        scale = gfull[:, feats]

        def tokens(k):
            rows = ds(k * 128, 128, 128)
            v = xv[rows, feats].astype(F32) * inv3(rows)
            v = (v * scale).astype(BF16).T
            for e in range(SUB // STRIP):
                strip = j * (SUB // STRIP) + e
                shard, nth = strip // STRIPS, strip % STRIPS
                to = ((shard // 4) * STRIPS + nth) * CHUNK + ((shard % 2) * 2 + (shard // 2) % 2) * STRIP
                out[ds(to, STRIP, 16), ds(at_lane + k * 128, 128, 128)] = v[e * STRIP:(e + 1) * STRIP]

        each(0, 4, tokens)

    def h_copy(j):
        rows = ds(j * CHUNK, CHUNK, CHUNK)
        return remote(hs.at[rows, :], ht.at[rows, own_tok], h_s.at[j], h_r.at[j], sib)

    def h_wait(j):
        rows = ds(j * CHUNK, CHUNK, CHUNK)
        remote(hs.at[rows, :], ht.at[rows, ds((1 - c) * TOK, TOK, TOK)], h_s.at[j], h_r.at[j], sib).wait_recv()

    def hidden_other(j):
        hidden_block(j, (1 - c) * HALF, hs, 0)

    def hidden_own(j):
        hidden_block(j, c * HALF, ht, c * TOK)

    odd = y % 2
    early, late = 3 * odd, 3 * (1 - odd)

    def chunk_of(i):
        return ((i // STRIPS + odd) % 2) * STRIPS + i % STRIPS

    each(0, 3, lambda j: hidden_other(early + j))
    each(0, STRIPS, lambda j: h_copy(chunk_of(j)).start())
    each(0, 3, lambda j: hidden_own(early + j))
    load_u.wait()
    remote(u_hbm, ups.at[ds((1 - c) * TOK, TOK, TOK), :], u_s, u_r, sib).wait_recv()

    rd[...] = jnp.zeros_like(rd)
    gsum[...] = jnp.zeros_like(gsum)

    def projection(d):
        for h in range(2):
            for k in range(2):
                arrive(w_half(d, zlo if k == 0 else 1 - zlo, 1 - c, h), wc_r.at[d, h, k])

    def delta(b):
        e = b // 3
        d = jnp.where(e == 2, 3, jnp.where(e == 3, 2, e))
        at = ((y + d) % 4) * 1152 + (b % 3) * SUB
        feats = ds(at, SUB, 128)
        sv[:, feats] = lax.dot_general(
            ups[own_tok, :], wv[ds(at, SUB, 32), :], (((1,), (1,)), ((), ())), preferred_element_type=F32
        )
        scale = gfull[:, feats]

        def tokens(k, col):
            rows = ds(k * 64, 64, 64)
            dl = sv[rows, feats]
            nm = xv[rows, feats].astype(F32) * inv3(rows)
            dn = dl * nm
            sn = dn * scale
            sv[rows, feats] = dl * scale
            rd[rows, :] = rd[rows, :] + (sn[:, :128] + sn[:, 128:256] + sn[:, 256:])
            return col + jnp.sum(dn.reshape(8, 8, SUB), axis=0)

        col = lax.fori_loop(0, 8, tokens, jnp.zeros((8, SUB), F32))
        gsum[:, feats] = jnp.sum(col, axis=0, keepdims=True)

    def finish(first, last):
        def block(j):
            rows = ds(j * 64, 64, 64)
            m = jnp.sum(rd[rows, :], axis=-1, keepdims=True) * (1.0 / D)
            m = jnp.broadcast_to(m, (64, 128))
            m = jnp.concatenate([m, m, m], axis=1)

            def part_of(k):
                feats = ds(k * SUB, SUB, 128)
                iv = inv3(rows)
                nm = xv[rows, feats].astype(F32) * iv
                ig[rows, feats] = (iv * (sv[rows, feats] - nm * m)).astype(BF16)

            each(0, 12, part_of)

        each(first, last, block)

    def gain_window(s):
        return ds(s * ROWS - (32 * s) % 128, 512, 128)

    def g1_copy(t):
        to = (me + t) % 16
        return remote(gsum.at[:, gain_window(to)], gone.at[me], g1_s.at[t], g1_r.at[t], (rep, to))

    def g1_wait(t):
        remote(gmine, gone.at[(me + 16 - t) % 16], g1_s.at[t], g1_r.at[t], sib).wait_recv()

    def g2_copy(t):
        return remote(gmine, gtwo.at[zhi], g2_s.at[t], g2_r.at[t], (((zhi + t) % 4) * 4 + x, me))

    def g2_wait(t):
        remote(gmine, gtwo.at[(zhi + 4 - t) % 4], g2_s.at[t], g2_r.at[t], sib).wait_recv()

    def g3_copy(t):
        return remote(gpart, gtwo.at[4 + x], g2_s.at[4 + t], g2_r.at[4 + t], (zhi * 4 + (x + t) % 4, me))

    def g3_wait(t):
        remote(gpart, gtwo.at[4 + (x + 4 - t) % 4], g2_s.at[4 + t], g2_r.at[4 + t], sib).wait_recv()

    def gain_first():
        each(1, 16, lambda t: g1_copy(t).start())
        gone[me] = gsum[:, gain_window(me)]

    def gain_second():
        each(1, 16, g1_wait)
        total = gone[0]
        for s in range(1, 16):
            total = total + gone[s]
        gmine[...] = total
        gtwo[zhi] = total
        each(1, 4, lambda t: g2_copy(t).start())

    def gain_third():
        each(1, 4, g2_wait)
        total = (gtwo[0] + gtwo[1]) + (gtwo[2] + gtwo[3])
        gpart[...] = total
        gtwo[4 + x] = total
        each(1, 4, lambda t: g3_copy(t).start())

    def gain_last():
        each(1, 4, g3_wait)
        total = (gtwo[4] + gtwo[5]) + (gtwo[6] + gtwo[7])
        total = jnp.broadcast_to(total * FACTOR, (8, 512))
        gg[...] = pltpu.roll(total, (512 - (32 * me) % 128) % 512, 1)[0, :ROWS]

    def s1_copy(j, h):
        return remote(s1.at[j, h], (l1 if h == 0 else r1).at[j], s1_s.at[j, h], s1_r.at[j, h], right if h == 0 else left)

    def s1_wait(j, h):
        remote(s1.at[j, h], (l1 if h == 0 else r1).at[j], s1_s.at[j, h], s1_r.at[j, h], left).wait_recv()

    def s2_copy(j, h):
        return remote(s2.at[j, h], (l2 if h == 0 else r2).at[j], s2_s.at[j, h], s2_r.at[j, h], right if h == 0 else left)

    def s2_wait(j, h):
        remote(s2.at[j, h], (l2 if h == 0 else r2).at[j], s2_s.at[j, h], s2_r.at[j, h], left).wait_recv()

    def matmul(j):
        h_wait(chunk_of(j))
        slot = j % HOLD
        rows = ds(chunk_of(j) * CHUNK, CHUNK, CHUNK)

        def quarter(q):
            return jnp.dot(ht[rows, :], ups[:, ds(q * QUART, QUART, 128)], preferred_element_type=F32)

        far = quarter((x + 2) % 4).astype(BF16)
        s1[j, 0] = far[:CHUNK // 2]
        s1[j, 1] = far[CHUNK // 2:]
        s1_copy(j, 0).start()
        s1_copy(j, 1).start()

        def near(q):
            part[slot, q] = quarter((x + jnp.where(q == 2, 3, q)) % 4)

        each(0, 3, near)

    def second(j):
        slot = j % HOLD
        mid = CHUNK // 2
        s1_wait(j, 0)
        s2[j, 0, :mid] = (part[slot, 1, :mid] + l1[j].astype(F32)).astype(BF16)
        s2[j, 0, mid:] = part[slot, 1, mid:].astype(BF16)
        s2_copy(j, 0).start()
        s1_wait(j, 1)
        s2[j, 1, :mid] = part[slot, 2, :mid].astype(BF16)
        s2[j, 1, mid:] = (part[slot, 2, mid:] + r1[j].astype(F32)).astype(BF16)
        s2_copy(j, 1).start()

    def s3_to(j):
        return 2 * c + (j // STRIPS + odd) % 2

    def s3_self(j, cc):
        return (s3_to(j) == y) & (cc == c)

    def s3_copy(j, cc):
        return remote(
            s3.at[j, cc], r3.at[j % STRIPS, y], s3_s.at[j, cc], s3_r.at[j % STRIPS, y], dev(x, s3_to(j), z, cc)
        )

    def third(j):
        slot = j % HOLD
        s2_wait(j, 0)
        s2_wait(j, 1)
        for cc in range(2):
            at = slice(cc * 2 * STRIP, (cc + 1) * 2 * STRIP)
            s3[j, cc] = part[slot, 0, at] + (l2[j, at].astype(F32) + r2[j, at].astype(F32))

            @pl.when(s3_self(j, cc))
            def _():
                pltpu.make_async_copy(s3.at[j, cc], r3.at[j % STRIPS, y], s3_r.at[j % STRIPS, y]).start()

            @pl.when(jnp.logical_not(s3_self(j, cc)))
            def _():
                s3_copy(j, cc).start()

    def z_send(n, zl, p):
        return remote(zs.at[n, zl, p], zr.at[n, z], z_s.at[n, zl, p], z_r.at[n, z], dev(x, y, 2 * p + zl, c))

    def fourth(n):
        for k in range(4):
            pltpu.make_async_copy(s3.at[0, 0], r3.at[n, k], s3_r.at[n, k]).wait()
        for zl in range(2):
            for h in range(2):
                at = slice(zl * STRIP + h * STRIP // 2, zl * STRIP + (h + 1) * STRIP // 2)
                total = (r3[n, 0, at] + r3[n, 1, at]) + (r3[n, 2, at] + r3[n, 3, at])
                zs[n, zl, 2 * h] = total[:, :128]
                zs[n, zl, 2 * h + 1] = total[:, 128:]

        def send(k):
            zl, p = k // 4, k % 4

            @pl.when(2 * p + zl == z)
            def _():
                pltpu.make_async_copy(zs.at[n, zl, p], zr.at[n, z], z_r.at[n, z]).start()

            @pl.when(2 * p + zl != z)
            def _():
                z_send(n, zl, p).start()

        each(0, 8, send)

    def a_copy(m, t):
        to = ((zhi + t) % 4) * 4 + x
        return remote(fb.at[m], ar.at[m, x, zhi], a_s.at[m, t], a_r.at[m, t], (to, me))

    def a_wait(m, t):
        remote(fb.at[m], ar.at[m, x, (zhi + 4 - t) % 4], a_s.at[m, t], a_r.at[m, t], sib).wait_recv()

    def b_copy(m, t):
        to = zhi * 4 + (x + t) % 4
        return remote(ar.at[m, x], ar.at[m, x], b_s.at[m, t], b_r.at[m, t], (to, me))

    def b_wait(m, t):
        src = (x + 4 - t) % 4
        remote(ar.at[m, src], ar.at[m, src], b_s.at[m, t], b_r.at[m, t], sib).wait_recv()

    def fifth(m):
        for e in range(2):
            n = 2 * m + e

            def wait(k):
                pltpu.make_async_copy(zs.at[0, 0, 0], zr.at[n, k], z_r.at[n, k]).wait()

            each(0, 8, wait)
        totals = []
        for e in range(2):
            total = zr[2 * m + e, 0]
            for k in range(1, 8):
                total = total + zr[2 * m + e, k]
            totals.append(total * FACTOR)
        both = jnp.concatenate(totals, axis=0).astype(BF16)
        fb[m] = both
        ar[m, x, zhi] = both
        each(1, 4, lambda t: a_copy(m, t).start())

    def sixth(m):
        each(1, 4, lambda t: a_wait(m, t))
        each(1, 4, lambda t: b_copy(m, t).start())

    def place(m):
        each(1, 4, lambda t: b_wait(m, t))
        for xs in range(4):
            for p in range(4):
                both = ar[m, xs, p].astype(F32)
                lanes = slice(QUART * xs + 128 * (p % 2), QUART * xs + 128 * (p % 2) + 128)
                for e in range(2):
                    rows = ds((2 * m + e) * STRIP + STRIP // 2 * (p // 2), STRIP // 2, 8)
                    wg[rows, lanes] = both[e * STRIP // 2:(e + 1) * STRIP // 2]

    def step(i):
        pl.when(i < CHUNKS)(lambda: matmul(i))
        pl.when((i >= 2) & (i < CHUNKS + 2))(lambda: second(i - 2))
        pl.when((i >= 4) & (i < CHUNKS + 4))(lambda: third(i - 4))
        n = i - 6 - STRIPS
        pl.when((n >= 0) & (n < STRIPS))(lambda: fourth(n))
        n = i - 8 - STRIPS
        pl.when((n >= 0) & (n < STRIPS) & (n % 2 == 1))(lambda: fifth(n // 2))
        n = i - 10 - STRIPS
        pl.when((n >= 0) & (n < STRIPS) & (n % 2 == 1))(lambda: sixth(n // 2))

        tasks = {
            0: [lambda: each(0, 2, lambda j: hidden_other(late + j))],
            1: [lambda: hidden_other(late + 2), lambda: each(STRIPS, CHUNKS, lambda j: h_copy(chunk_of(j)).start()),
                lambda: w_near(0, 0), lambda: w_near(1, 0), lambda: w_other(0, 0), lambda: w_other(0, 1),
                lambda: hidden_own(late)],
            2: [lambda: hidden_own(late + 1)],
            3: [lambda: hidden_own(late + 2)],
            4: [lambda: w_near(0, 1), lambda: w_near(1, 1), lambda: projection(0)],
            6: [lambda: w_far(0), lambda: w_far(1), lambda: w_other(3, 0), lambda: w_other(1, 1)],
            8: [lambda: w_other(1, 0), lambda: w_other(3, 1)],
            9: [lambda: projection(1)],
            10: [lambda: w_other(2, 0), lambda: w_other(2, 1), lambda: projection(3)],
            12: [lambda: projection(2)],
            15: [gain_first],
            17: [gain_second],
            20: [gain_third, lambda: place(0)],
            21: [lambda: place(1)],
        }
        for at, todo in tasks.items():
            def run(todo=todo):
                for task in todo:
                    task()

            pl.when(i == at)(run)

        pl.when(((i >= 4) & (i < 7)) | ((i >= 9) & (i < 15)))(
            lambda: delta(jnp.where(i < 7, i - 4, jnp.where(i < 12, 2 * i - 15, i - 3)))
        )
        pl.when((i >= 9) & (i < 12))(lambda: delta(2 * i - 14))
        pl.when((i >= 16) & (i < 20))(lambda: finish(2 * (i - 16), 2 * (i - 16) + 2))

    each(0, CHUNKS + 10, step)

    def sent(t):
        gain_copy(t).wait_send()
        g1_copy(t).wait_send()

    each(1, 16, sent)
    u_copy.wait_send()
    each(0, CHUNKS, lambda j: h_copy(j).wait_send())
    for way in range(2):
        for h in range(2):
            y_own(way, h).wait_send()
        y_pass(way).wait_send()
    for d in range(4):
        for h in range(2):
            z_half(d, h).wait_send()
            for k in range(2):
                c_half(d, h, k).wait_send()

    def sums_sent(j):
        for h in range(2):
            s1_copy(j, h).wait_send()
            s2_copy(j, h).wait_send()
            pl.when(jnp.logical_not(s3_self(j, h)))(lambda h=h: s3_copy(j, h).wait_send())

    each(0, CHUNKS, sums_sent)

    def z_sent(k):
        n, zl, p = k // 8, (k // 4) % 2, k % 4
        pl.when(2 * p + zl != z)(lambda: z_send(n, zl, p).wait_send())

    each(0, 8 * STRIPS, z_sent)

    gain_last()
    place(2)

    def gains_sent(t):
        g2_copy(t).wait_send()
        g3_copy(t).wait_send()

    each(1, 4, gains_sent)

    def replicas_sent(m):
        def one(t):
            a_copy(m, t).wait_send()
            b_copy(m, t).wait_send()

        each(1, 4, one)

    each(0, STRIPS // 2, replicas_sent)


def hand_out(ig, wg, gg, ig_hbm, wg_hbm, gg_hbm, sems):
    copies = [pltpu.make_async_copy(ig.at[pl.ds(k * 64, 64)], ig_hbm.at[pl.ds(k * 64, 64)], sems.at[k]) for k in range(8)]
    copies += [pltpu.make_async_copy(wg, wg_hbm, sems.at[8]), pltpu.make_async_copy(gg, gg_hbm, sems.at[9])]
    for copy in copies:
        copy.start()
    for copy in copies:
        copy.wait()


def local(inputs, gain, weight, upstream):
    vmem = pltpu.VMEM
    dma = pltpu.SemaphoreType.DMA
    anywhere = pl.BlockSpec(memory_space=pl.ANY)
    whole = pl.BlockSpec(memory_space=pltpu.VMEM)
    input_grad, weight_grad, gain_grad = pl.pallas_call(
        kernel,
        out_shape=(
            vmem((TOK, D), BF16),
            vmem((ROWS, COLS), F32),
            vmem((ROWS,), F32),
        ),
        in_specs=[anywhere] * 4,
        out_specs=(whole, whole, whole),
        scratch_shapes=[
            vmem((TOK, D), BF16),
            vmem((D, COLS), BF16),
            vmem((TOK, D), F32),
            vmem((HALF, 2 * TOK), BF16),
            vmem((HALF, TOK), BF16),
            vmem((2 * TOK, COLS), BF16),
            vmem((TOK, 128), F32),
            vmem((TOK, 128), F32),
            vmem((1, PAD), F32),
            vmem((1, PAD), F32),
            vmem((16, 1, 512), F32),
            vmem((16, 1, 512), F32),
            vmem((8, 1, 512), F32),
            vmem((1, 512), F32),
            vmem((1, 512), F32),
            vmem((1, 512), F32),
            vmem((ROWS,), BF16),
            vmem((HOLD, 3, CHUNK, QUART), F32),
            vmem((CHUNKS, 2, CHUNK // 2, QUART), BF16),
            vmem((CHUNKS, CHUNK // 2, QUART), BF16),
            vmem((CHUNKS, CHUNK // 2, QUART), BF16),
            vmem((CHUNKS, 2, CHUNK, QUART), BF16),
            vmem((CHUNKS, CHUNK, QUART), BF16),
            vmem((CHUNKS, CHUNK, QUART), BF16),
            vmem((CHUNKS, 2, CHUNK // 2, QUART), F32),
            vmem((STRIPS, 4, CHUNK // 2, QUART), F32),
            vmem((STRIPS, 2, 4, STRIP // 2, 128), F32),
            vmem((STRIPS, 8, STRIP // 2, 128), F32),
            vmem((STRIPS // 2, STRIP, 128), BF16),
            vmem((STRIPS // 2, 4, 4, STRIP, 128), BF16),
            dma, dma((8,)), dma, dma,
            dma((16,)), dma((16,)), dma((16,)), dma((16,)), dma((8,)), dma((8,)),
            dma, dma, dma((CHUNKS,)), dma((CHUNKS,)),
            dma((3, 2)), dma((3, 2)), dma((4, 2)), dma((4, 2)), dma((4, 2, 2)), dma((4, 2, 2)),
            dma((CHUNKS, 2)), dma((CHUNKS, 2)), dma((CHUNKS, 2)), dma((CHUNKS, 2)), dma((CHUNKS, 2)), dma((STRIPS, 4)),
            dma((STRIPS, 2, 4)), dma((STRIPS, 8)),
            dma((STRIPS // 2, 4)), dma((STRIPS // 2, 4)), dma((STRIPS // 2, 4)), dma((STRIPS // 2, 4)),
        ],
        compiler_params=pltpu.CompilerParams(
            collective_id=0, has_side_effects=True, vmem_limit_bytes=54 << 20
        ),
        name="backward",
    )(inputs, gain, weight, upstream)
    held = [pltpu.with_memory_space_constraint(a, pltpu.VMEM) for a in (input_grad, weight_grad, gain_grad)]
    return pl.pallas_call(
        hand_out,
        out_shape=tuple(jax.ShapeDtypeStruct(a.shape, a.dtype) for a in held),
        in_specs=[whole] * 3,
        out_specs=(anywhere,) * 3,
        scratch_shapes=[dma((10,))],
        compiler_params=pltpu.CompilerParams(vmem_limit_bytes=1 << 20),
        name="hand_out",
    )(*held)


def solution(mesh):
    return jax.shard_map(
        local,
        mesh=mesh,
        in_specs=(
            P(("rep", "shard"), None),
            P("shard"),
            P("shard", None),
            P(("rep", "shard"), None),
        ),
        out_specs=(P(("rep", "shard"), None), P("shard", None), P("shard")),
        check_vma=False,
    )
```

```python
import math

import jax
import jax.numpy as jnp
from jax import lax
from jax.experimental import pallas as pl
from jax.experimental.pallas import tpu as pltpu
from jax.sharding import PartitionSpec as P

MESH = pl.DeviceIdType.MESH
F32 = jnp.float32
BF16 = jnp.bfloat16
TOK = 512
D = 4608
COLS = 1024
ROWS = 288
HALF = D // 2
SUB = 384
QUART = COLS // 4
PAD = D + 128
STRIP = 48
CHUNK = 4 * STRIP
CHUNKS = HALF // CHUNK
STRIPS = ROWS // STRIP
HOLD = 5
FACTOR = 1.0 / math.sqrt(131072)


def ds(start, size, unit):
    return pl.ds(pl.multiple_of(start, unit), size)


def remote(src, dst, send, recv, device):
    return pltpu.make_async_remote_copy(
        src_ref=src, dst_ref=dst, send_sem=send, recv_sem=recv, device_id=device, device_id_type=MESH
    )


def each(first, last, step):
    def body(t, carry):
        step(t)
        return carry

    lax.fori_loop(first, last, body, 0)


def kernel(
    x_hbm, gain_hbm, w_hbm, u_hbm,
    ig, wg, gg,
    xv, wv, sv, ht, hs, ups, inv, rd, gfull, gsum, gbuf, gone, gtwo, gmine, gpart, win, gain,
    part, s1, l1, r1, s2, l2, r2, s3, r3, zs, zr, fb, ar,
    ld_g, ld_x, ld_u, ld_w,
    gb_s, gb_r, g1_s, g1_r, g2_s, g2_r,
    u_s, u_r, h_s, h_r,
    wy_s, wy_r, wz_s, wz_r, wc_s, wc_r,
    s1_s, s1_r, s2_s, s2_r, s3_s, s3_r, z_s, z_r, a_s, a_r, b_s, b_r,
):
    rep = lax.axis_index("rep")
    me = lax.axis_index("shard")
    x, zhi = rep % 4, rep // 4
    y, zlo, c = me // 4, (me // 2) % 2, me % 2
    z = zhi * 2 + zlo

    def dev(xx, yy, zz, cc):
        return ((zz // 2) * 4 + xx, (yy * 2 + zz % 2) * 2 + cc)

    sib = (rep, me + 1 - 2 * c)
    right, left = dev((x + 1) % 4, y, z, c), dev((x + 3) % 4, y, z, c)
    up, down = dev(x, y, (z + 1) % 8, c), dev(x, y, (z + 7) % 8, c)

    barrier = pltpu.get_barrier_semaphore()

    def hello(device):
        pl.semaphore_signal(barrier, inc=1, device_id=device, device_id_type=MESH)

    each(1, 16, lambda t: hello((rep, (me + t) % 16)))

    def hello_far(t):
        far = ((zhi + t) % 4) * 4 + x
        hello((far, me))
        hello((far, (y * 2 + 1 - zlo) * 2 + c))
        hello((zhi * 4 + (x + t) % 4, me))

    each(1, 4, hello_far)

    load_g = pltpu.make_async_copy(gain_hbm, gain, ld_g)
    load_g.start()

    def load_x(k):
        rows = ds(k * 64, 64, 64)
        return pltpu.make_async_copy(x_hbm.at[rows, :], xv.at[rows, :], ld_x.at[k])

    each(0, 8, lambda k: load_x(k).start())
    own_tok = ds(c * TOK, TOK, TOK)
    load_u = pltpu.make_async_copy(u_hbm, ups.at[own_tok, :], ld_u)
    load_u.start()
    own_rows = ds(me * ROWS, ROWS, 32)
    load_w = pltpu.make_async_copy(w_hbm, wv.at[own_rows, :], ld_w)
    load_w.start()

    load_g.wait()
    row = jnp.concatenate([gain[...].astype(F32).reshape(1, ROWS), jnp.zeros((1, 512 - ROWS), F32)], axis=1)
    win[...] = pltpu.roll(jnp.broadcast_to(row, (8, 512)), (32 * me) % 128, 1)[:1]

    pl.semaphore_wait(barrier, 24)

    def gain_copy(t):
        return remote(win, gbuf.at[me], gb_s.at[t], gb_r.at[t], (rep, (me + t) % 16))

    each(1, 16, lambda t: gain_copy(t).start())
    gbuf[me] = win[...]
    u_copy = remote(u_hbm, ups.at[own_tok, :], u_s, u_r, sib)
    u_copy.start()

    def w_half(d, zl, cc, h):
        return ds(((((y + d) % 4) * 2 + zl) * 2 + cc) * ROWS + h * 144, 144, 16)

    def y_own(way, h):
        rows = w_half(0, zlo, c, h)
        to = dev(x, (y + (1 if way == 0 else 3)) % 4, z, c)
        return remote(wv.at[rows, :], wv.at[rows, :], wy_s.at[way, h], wy_r.at[way, h], to)

    def y_pass(way):
        rows = w_half(3 if way == 0 else 1, zlo, c, way)
        to = dev(x, (y + (1 if way == 0 else 3)) % 4, z, c)
        return remote(wv.at[rows, :], wv.at[rows, :], wy_s.at[2, way], wy_r.at[2, way], to)

    def z_half(d, h):
        rows = w_half(d, zlo, c, h)
        return remote(wv.at[rows, :], wv.at[rows, :], wz_s.at[d, h], wz_r.at[d, h], up if h == 0 else down)

    def c_half(d, h, k):
        rows = w_half(d, zlo if k == 0 else 1 - zlo, c, h)
        return remote(wv.at[rows, :], wv.at[rows, :], wc_s.at[d, h, k], wc_r.at[d, h, k], sib)

    def arrive(rows, sem):
        remote(wv.at[rows, :], wv.at[rows, :], wc_s.at[0, 0, 0], sem, sib).wait_recv()

    def w_have(d, h):
        z_half(d, h).start()
        c_half(d, h, 0).start()

    def w_near(h, k):
        way = h if k == 0 else 1 - h
        d = 3 if way == 0 else 1
        arrive(w_half(d, zlo, c, h), wy_r.at[way, h])
        if k == 0:
            y_pass(way).start()
        w_have(d, h)

    def w_far(h):
        arrive(w_half(2, zlo, c, h), wy_r.at[2, h])
        w_have(2, h)

    def w_other(d, h):
        arrive(w_half(d, 1 - zlo, c, h), wz_r.at[d, h])
        c_half(d, h, 1).start()

    load_w.wait()
    for way in (0, 1):
        y_own(way, way).start()
        w_have(0, way)
    for way in (0, 1):
        y_own(way, 1 - way).start()

    def norm_block(k):
        load_x(k).wait()
        rows = ds(k * 64, 64, 64)
        total = jnp.zeros((64, 128), F32)
        for j in range(D // 512):
            v = xv[rows, j * 512:(j + 1) * 512].astype(F32)
            v = v * v
            total = total + ((v[:, :128] + v[:, 128:256]) + (v[:, 256:384] + v[:, 384:]))
        mean = jnp.sum(total, axis=-1, keepdims=True) * (1.0 / D)
        inv[rows, :] = jnp.broadcast_to(lax.rsqrt(mean + 1e-06), (64, 128))

    each(0, 8, norm_block)

    def gain_wait(t):
        remote(win, gbuf.at[(me + 16 - t) % 16], gb_s.at[t], gb_r.at[t], sib).wait_recv()

    each(1, 16, gain_wait)
    gfull[...] = jnp.ones((1, PAD), F32)
    for s in range(16):
        at = (ROWS * s) // 128 * 128
        gfull[:, at:at + 512] = gfull[:, at:at + 512] + gbuf[s]

    def inv3(rows):
        iv = inv[rows, :]
        return jnp.concatenate([iv, iv, iv], axis=1)

    def hidden_block(j, at_feature, out, at_lane):
        feats = ds(at_feature + j * SUB, SUB, 128)
        scale = gfull[:, feats]

        def tokens(k):
            rows = ds(k * 128, 128, 128)
            v = xv[rows, feats].astype(F32) * inv3(rows)
            v = (v * scale).astype(BF16).T
            for e in range(SUB // STRIP):
                strip = j * (SUB // STRIP) + e
                shard, nth = strip // STRIPS, strip % STRIPS
                to = ((shard // 4) * STRIPS + nth) * CHUNK + ((shard % 2) * 2 + (shard // 2) % 2) * STRIP
                out[ds(to, STRIP, 16), ds(at_lane + k * 128, 128, 128)] = v[e * STRIP:(e + 1) * STRIP]

        each(0, 4, tokens)

    def h_copy(j):
        rows = ds(j * CHUNK, CHUNK, CHUNK)
        return remote(hs.at[rows, :], ht.at[rows, own_tok], h_s.at[j], h_r.at[j], sib)

    def h_wait(j):
        rows = ds(j * CHUNK, CHUNK, CHUNK)
        remote(hs.at[rows, :], ht.at[rows, ds((1 - c) * TOK, TOK, TOK)], h_s.at[j], h_r.at[j], sib).wait_recv()

    def hidden_other(j):
        hidden_block(j, (1 - c) * HALF, hs, 0)

    def hidden_own(j):
        hidden_block(j, c * HALF, ht, c * TOK)

    odd = y % 2
    early, late = 3 * odd, 3 * (1 - odd)

    def chunk_of(i):
        return ((i // STRIPS + odd) % 2) * STRIPS + i % STRIPS

    each(0, 3, lambda j: hidden_other(early + j))
    each(0, STRIPS, lambda j: h_copy(chunk_of(j)).start())
    each(0, 3, lambda j: hidden_own(early + j))
    load_u.wait()
    remote(u_hbm, ups.at[ds((1 - c) * TOK, TOK, TOK), :], u_s, u_r, sib).wait_recv()

    rd[...] = jnp.zeros_like(rd)
    gsum[...] = jnp.zeros_like(gsum)

    def projection(d):
        for h in range(2):
            for k in range(2):
                arrive(w_half(d, zlo if k == 0 else 1 - zlo, 1 - c, h), wc_r.at[d, h, k])

    def delta(b):
        e = b // 3
        d = jnp.where(e == 2, 3, jnp.where(e == 3, 2, e))
        at = ((y + d) % 4) * 1152 + (b % 3) * SUB
        feats = ds(at, SUB, 128)
        sv[:, feats] = lax.dot_general(
            ups[own_tok, :], wv[ds(at, SUB, 32), :], (((1,), (1,)), ((), ())), preferred_element_type=F32
        )
        scale = gfull[:, feats]

        def tokens(k, col):
            rows = ds(k * 64, 64, 64)
            dl = sv[rows, feats]
            nm = xv[rows, feats].astype(F32) * inv3(rows)
            dn = dl * nm
            sn = dn * scale
            sv[rows, feats] = dl * scale
            rd[rows, :] = rd[rows, :] + (sn[:, :128] + sn[:, 128:256] + sn[:, 256:])
            return col + jnp.sum(dn.reshape(8, 8, SUB), axis=0)

        col = lax.fori_loop(0, 8, tokens, jnp.zeros((8, SUB), F32))
        gsum[:, feats] = jnp.sum(col, axis=0, keepdims=True)

    def finish(first, last):
        def block(j):
            rows = ds(j * 64, 64, 64)
            m = jnp.sum(rd[rows, :], axis=-1, keepdims=True) * (1.0 / D)
            m = jnp.broadcast_to(m, (64, 128))
            m = jnp.concatenate([m, m, m], axis=1)

            def part_of(k):
                feats = ds(k * SUB, SUB, 128)
                iv = inv3(rows)
                nm = xv[rows, feats].astype(F32) * iv
                ig[rows, feats] = (iv * (sv[rows, feats] - nm * m)).astype(BF16)

            each(0, 12, part_of)

        each(first, last, block)

    def gain_window(s):
        return ds(s * ROWS - (32 * s) % 128, 512, 128)

    def g1_copy(t):
        to = (me + t) % 16
        return remote(gsum.at[:, gain_window(to)], gone.at[me], g1_s.at[t], g1_r.at[t], (rep, to))

    def g1_wait(t):
        remote(gmine, gone.at[(me + 16 - t) % 16], g1_s.at[t], g1_r.at[t], sib).wait_recv()

    def g2_copy(t):
        return remote(gmine, gtwo.at[zhi], g2_s.at[t], g2_r.at[t], (((zhi + t) % 4) * 4 + x, me))

    def g2_wait(t):
        remote(gmine, gtwo.at[(zhi + 4 - t) % 4], g2_s.at[t], g2_r.at[t], sib).wait_recv()

    def g3_copy(t):
        return remote(gpart, gtwo.at[4 + x], g2_s.at[4 + t], g2_r.at[4 + t], (zhi * 4 + (x + t) % 4, me))

    def g3_wait(t):
        remote(gpart, gtwo.at[4 + (x + 4 - t) % 4], g2_s.at[4 + t], g2_r.at[4 + t], sib).wait_recv()

    def gain_first():
        each(1, 16, lambda t: g1_copy(t).start())
        gone[me] = gsum[:, gain_window(me)]

    def gain_second():
        each(1, 16, g1_wait)
        total = gone[0]
        for s in range(1, 16):
            total = total + gone[s]
        gmine[...] = total
        gtwo[zhi] = total
        each(1, 4, lambda t: g2_copy(t).start())

    def gain_third():
        each(1, 4, g2_wait)
        total = (gtwo[0] + gtwo[1]) + (gtwo[2] + gtwo[3])
        gpart[...] = total
        gtwo[4 + x] = total
        each(1, 4, lambda t: g3_copy(t).start())

    def gain_last():
        each(1, 4, g3_wait)
        total = (gtwo[4] + gtwo[5]) + (gtwo[6] + gtwo[7])
        total = jnp.broadcast_to(total * FACTOR, (8, 512))
        gg[...] = pltpu.roll(total, (512 - (32 * me) % 128) % 512, 1)[0, :ROWS]

    def s1_copy(j, h):
        return remote(s1.at[j, h], (l1 if h == 0 else r1).at[j], s1_s.at[j, h], s1_r.at[j, h], right if h == 0 else left)

    def s1_wait(j, h):
        remote(s1.at[j, h], (l1 if h == 0 else r1).at[j], s1_s.at[j, h], s1_r.at[j, h], left).wait_recv()

    def s2_copy(j, h):
        return remote(s2.at[j, h], (l2 if h == 0 else r2).at[j], s2_s.at[j, h], s2_r.at[j, h], right if h == 0 else left)

    def s2_wait(j, h):
        remote(s2.at[j, h], (l2 if h == 0 else r2).at[j], s2_s.at[j, h], s2_r.at[j, h], left).wait_recv()

    def matmul(j):
        h_wait(chunk_of(j))
        slot = j % HOLD
        rows = ds(chunk_of(j) * CHUNK, CHUNK, CHUNK)

        def quarter(q):
            return jnp.dot(ht[rows, :], ups[:, ds(q * QUART, QUART, 128)], preferred_element_type=F32)

        far = quarter((x + 2) % 4).astype(BF16)
        s1[j, 0] = far[:CHUNK // 2]
        s1[j, 1] = far[CHUNK // 2:]
        s1_copy(j, 0).start()
        s1_copy(j, 1).start()

        def near(q):
            part[slot, q] = quarter((x + jnp.where(q == 2, 3, q)) % 4)

        each(0, 3, near)

    def second(j):
        slot = j % HOLD
        mid = CHUNK // 2
        s1_wait(j, 0)
        s2[j, 0, :mid] = (part[slot, 1, :mid] + l1[j].astype(F32)).astype(BF16)
        s2[j, 0, mid:] = part[slot, 1, mid:].astype(BF16)
        s2_copy(j, 0).start()
        s1_wait(j, 1)
        s2[j, 1, :mid] = part[slot, 2, :mid].astype(BF16)
        s2[j, 1, mid:] = (part[slot, 2, mid:] + r1[j].astype(F32)).astype(BF16)
        s2_copy(j, 1).start()

    def s3_to(j):
        return 2 * c + (j // STRIPS + odd) % 2

    def s3_self(j, cc):
        return (s3_to(j) == y) & (cc == c)

    def s3_copy(j, cc):
        return remote(
            s3.at[j, cc], r3.at[j % STRIPS, y], s3_s.at[j, cc], s3_r.at[j % STRIPS, y], dev(x, s3_to(j), z, cc)
        )

    def third(j):
        slot = j % HOLD
        s2_wait(j, 0)
        s2_wait(j, 1)
        for cc in range(2):
            at = slice(cc * 2 * STRIP, (cc + 1) * 2 * STRIP)
            s3[j, cc] = part[slot, 0, at] + (l2[j, at].astype(F32) + r2[j, at].astype(F32))

            @pl.when(s3_self(j, cc))
            def _():
                pltpu.make_async_copy(s3.at[j, cc], r3.at[j % STRIPS, y], s3_r.at[j % STRIPS, y]).start()

            @pl.when(jnp.logical_not(s3_self(j, cc)))
            def _():
                s3_copy(j, cc).start()

    def z_send(n, zl, p):
        return remote(zs.at[n, zl, p], zr.at[n, z], z_s.at[n, zl, p], z_r.at[n, z], dev(x, y, 2 * p + zl, c))

    def fourth(n):
        for k in range(4):
            pltpu.make_async_copy(s3.at[0, 0], r3.at[n, k], s3_r.at[n, k]).wait()
        for zl in range(2):
            for h in range(2):
                at = slice(zl * STRIP + h * STRIP // 2, zl * STRIP + (h + 1) * STRIP // 2)
                total = (r3[n, 0, at] + r3[n, 1, at]) + (r3[n, 2, at] + r3[n, 3, at])
                zs[n, zl, 2 * h] = total[:, :128]
                zs[n, zl, 2 * h + 1] = total[:, 128:]

        def send(k):
            zl, p = k // 4, k % 4

            @pl.when(2 * p + zl == z)
            def _():
                pltpu.make_async_copy(zs.at[n, zl, p], zr.at[n, z], z_r.at[n, z]).start()

            @pl.when(2 * p + zl != z)
            def _():
                z_send(n, zl, p).start()

        each(0, 8, send)

    def a_copy(m, t):
        to = ((zhi + t) % 4) * 4 + x
        return remote(fb.at[m], ar.at[m, x, zhi], a_s.at[m, t], a_r.at[m, t], (to, me))

    def a_wait(m, t):
        remote(fb.at[m], ar.at[m, x, (zhi + 4 - t) % 4], a_s.at[m, t], a_r.at[m, t], sib).wait_recv()

    def b_copy(m, t):
        to = zhi * 4 + (x + t) % 4
        return remote(ar.at[m, x], ar.at[m, x], b_s.at[m, t], b_r.at[m, t], (to, me))

    def b_wait(m, t):
        src = (x + 4 - t) % 4
        remote(ar.at[m, src], ar.at[m, src], b_s.at[m, t], b_r.at[m, t], sib).wait_recv()

    def fifth(m):
        for e in range(2):
            n = 2 * m + e

            def wait(k):
                pltpu.make_async_copy(zs.at[0, 0, 0], zr.at[n, k], z_r.at[n, k]).wait()

            each(0, 8, wait)
        totals = []
        for e in range(2):
            total = zr[2 * m + e, 0]
            for k in range(1, 8):
                total = total + zr[2 * m + e, k]
            totals.append(total * FACTOR)
        both = jnp.concatenate(totals, axis=0).astype(BF16)
        fb[m] = both
        ar[m, x, zhi] = both
        each(1, 4, lambda t: a_copy(m, t).start())

    def sixth(m):
        each(1, 4, lambda t: a_wait(m, t))
        each(1, 4, lambda t: b_copy(m, t).start())

    def place(m):
        each(1, 4, lambda t: b_wait(m, t))
        for xs in range(4):
            for p in range(4):
                both = ar[m, xs, p].astype(F32)
                lanes = slice(QUART * xs + 128 * (p % 2), QUART * xs + 128 * (p % 2) + 128)
                for e in range(2):
                    rows = ds((2 * m + e) * STRIP + STRIP // 2 * (p // 2), STRIP // 2, 8)
                    wg[rows, lanes] = both[e * STRIP // 2:(e + 1) * STRIP // 2]

    def step(i):
        pl.when(i < CHUNKS)(lambda: matmul(i))
        pl.when((i >= 2) & (i < CHUNKS + 2))(lambda: second(i - 2))
        pl.when((i >= 4) & (i < CHUNKS + 4))(lambda: third(i - 4))
        n = i - 6 - STRIPS
        pl.when((n >= 0) & (n < STRIPS))(lambda: fourth(n))
        n = i - 8 - STRIPS
        pl.when((n >= 0) & (n < STRIPS) & (n % 2 == 1))(lambda: fifth(n // 2))
        n = i - 10 - STRIPS
        pl.when((n >= 0) & (n < STRIPS) & (n % 2 == 1))(lambda: sixth(n // 2))

        tasks = {
            1: [lambda: w_near(0, 0), lambda: w_near(1, 0)],
            2: [lambda: hidden_other(late), lambda: w_other(0, 0), lambda: w_other(0, 1)],
            3: [lambda: hidden_other(late + 1), lambda: hidden_other(late + 2),
                lambda: each(STRIPS, CHUNKS, lambda j: h_copy(chunk_of(j)).start())],
            4: [lambda: hidden_own(late), lambda: w_near(0, 1), lambda: w_near(1, 1), lambda: projection(0)],
            5: [lambda: hidden_own(late + 1), lambda: hidden_own(late + 2)],
            6: [lambda: w_far(0), lambda: w_far(1), lambda: w_other(3, 0), lambda: w_other(1, 1)],
            8: [lambda: w_other(1, 0), lambda: w_other(3, 1)],
            9: [lambda: projection(1)],
            10: [lambda: w_other(2, 0), lambda: w_other(2, 1), lambda: projection(3)],
            12: [lambda: projection(2)],
            15: [gain_first],
            17: [gain_second],
            20: [gain_third, lambda: place(0)],
            21: [lambda: place(1)],
        }
        for at, todo in tasks.items():
            def run(todo=todo):
                for task in todo:
                    task()

            pl.when(i == at)(run)

        pl.when((i >= 6) & (i < 15))(
            lambda: delta(jnp.where(i < 9, i - 6, jnp.where(i < 12, 2 * i - 15, i - 3)))
        )
        pl.when((i >= 9) & (i < 12))(lambda: delta(2 * i - 14))
        pl.when((i >= 16) & (i < 20))(lambda: finish(2 * (i - 16), 2 * (i - 16) + 2))

    each(0, CHUNKS + 10, step)

    def sent(t):
        gain_copy(t).wait_send()
        g1_copy(t).wait_send()

    each(1, 16, sent)
    u_copy.wait_send()
    each(0, CHUNKS, lambda j: h_copy(j).wait_send())
    for way in range(2):
        for h in range(2):
            y_own(way, h).wait_send()
        y_pass(way).wait_send()
    for d in range(4):
        for h in range(2):
            z_half(d, h).wait_send()
            for k in range(2):
                c_half(d, h, k).wait_send()

    def sums_sent(j):
        for h in range(2):
            s1_copy(j, h).wait_send()
            s2_copy(j, h).wait_send()
            pl.when(jnp.logical_not(s3_self(j, h)))(lambda h=h: s3_copy(j, h).wait_send())

    each(0, CHUNKS, sums_sent)

    def z_sent(k):
        n, zl, p = k // 8, (k // 4) % 2, k % 4
        pl.when(2 * p + zl != z)(lambda: z_send(n, zl, p).wait_send())

    each(0, 8 * STRIPS, z_sent)

    gain_last()
    place(2)

    def gains_sent(t):
        g2_copy(t).wait_send()
        g3_copy(t).wait_send()

    each(1, 4, gains_sent)

    def replicas_sent(m):
        def one(t):
            a_copy(m, t).wait_send()
            b_copy(m, t).wait_send()

        each(1, 4, one)

    each(0, STRIPS // 2, replicas_sent)


def hand_out(ig, wg, gg, ig_hbm, wg_hbm, gg_hbm, sems):
    copies = [pltpu.make_async_copy(ig.at[pl.ds(k * 64, 64)], ig_hbm.at[pl.ds(k * 64, 64)], sems.at[k]) for k in range(8)]
    copies += [pltpu.make_async_copy(wg, wg_hbm, sems.at[8]), pltpu.make_async_copy(gg, gg_hbm, sems.at[9])]
    for copy in copies:
        copy.start()
    for copy in copies:
        copy.wait()


def local(inputs, gain, weight, upstream):
    vmem = pltpu.VMEM
    dma = pltpu.SemaphoreType.DMA
    anywhere = pl.BlockSpec(memory_space=pl.ANY)
    whole = pl.BlockSpec(memory_space=pltpu.VMEM)
    input_grad, weight_grad, gain_grad = pl.pallas_call(
        kernel,
        out_shape=(
            vmem((TOK, D), BF16),
            vmem((ROWS, COLS), F32),
            vmem((ROWS,), F32),
        ),
        in_specs=[anywhere] * 4,
        out_specs=(whole, whole, whole),
        scratch_shapes=[
            vmem((TOK, D), BF16),
            vmem((D, COLS), BF16),
            vmem((TOK, D), F32),
            vmem((HALF, 2 * TOK), BF16),
            vmem((HALF, TOK), BF16),
            vmem((2 * TOK, COLS), BF16),
            vmem((TOK, 128), F32),
            vmem((TOK, 128), F32),
            vmem((1, PAD), F32),
            vmem((1, PAD), F32),
            vmem((16, 1, 512), F32),
            vmem((16, 1, 512), F32),
            vmem((8, 1, 512), F32),
            vmem((1, 512), F32),
            vmem((1, 512), F32),
            vmem((1, 512), F32),
            vmem((ROWS,), BF16),
            vmem((HOLD, 3, CHUNK, QUART), F32),
            vmem((CHUNKS, 2, CHUNK // 2, QUART), BF16),
            vmem((CHUNKS, CHUNK // 2, QUART), BF16),
            vmem((CHUNKS, CHUNK // 2, QUART), BF16),
            vmem((CHUNKS, 2, CHUNK, QUART), BF16),
            vmem((CHUNKS, CHUNK, QUART), BF16),
            vmem((CHUNKS, CHUNK, QUART), BF16),
            vmem((CHUNKS, 2, CHUNK // 2, QUART), F32),
            vmem((STRIPS, 4, CHUNK // 2, QUART), F32),
            vmem((STRIPS, 2, 4, STRIP // 2, 128), F32),
            vmem((STRIPS, 8, STRIP // 2, 128), F32),
            vmem((STRIPS // 2, STRIP, 128), BF16),
            vmem((STRIPS // 2, 4, 4, STRIP, 128), BF16),
            dma, dma((8,)), dma, dma,
            dma((16,)), dma((16,)), dma((16,)), dma((16,)), dma((8,)), dma((8,)),
            dma, dma, dma((CHUNKS,)), dma((CHUNKS,)),
            dma((3, 2)), dma((3, 2)), dma((4, 2)), dma((4, 2)), dma((4, 2, 2)), dma((4, 2, 2)),
            dma((CHUNKS, 2)), dma((CHUNKS, 2)), dma((CHUNKS, 2)), dma((CHUNKS, 2)), dma((CHUNKS, 2)), dma((STRIPS, 4)),
            dma((STRIPS, 2, 4)), dma((STRIPS, 8)),
            dma((STRIPS // 2, 4)), dma((STRIPS // 2, 4)), dma((STRIPS // 2, 4)), dma((STRIPS // 2, 4)),
        ],
        compiler_params=pltpu.CompilerParams(
            collective_id=0, has_side_effects=True, vmem_limit_bytes=54 << 20
        ),
        name="backward",
    )(inputs, gain, weight, upstream)
    held = [pltpu.with_memory_space_constraint(a, pltpu.VMEM) for a in (input_grad, weight_grad, gain_grad)]
    return pl.pallas_call(
        hand_out,
        out_shape=tuple(jax.ShapeDtypeStruct(a.shape, a.dtype) for a in held),
        in_specs=[whole] * 3,
        out_specs=(anywhere,) * 3,
        scratch_shapes=[dma((10,))],
        compiler_params=pltpu.CompilerParams(vmem_limit_bytes=1 << 20),
        name="hand_out",
    )(*held)


def solution(mesh):
    return jax.shard_map(
        local,
        mesh=mesh,
        in_specs=(
            P(("rep", "shard"), None),
            P("shard"),
            P("shard", None),
            P(("rep", "shard"), None),
        ),
        out_specs=(P(("rep", "shard"), None), P("shard", None), P("shard")),
        check_vma=False,
    )
```
